32 devices in a mesh: grp: 2 (over y), col: 16 (over z, x, core).
Axes of the slice: x: 2, y: 2, z: 4, core: 2. Of those that a mesh axis runs over, the one named last changes fastest.
Arguments:
- doc_factors: float32 [1024, 256], P(('grp', 'col')), may hold values from -1.5 to 1.5
- ngram_factors: float32 [8192, 256], P('col'), may hold values from -1.5 to 1.5
- block_docs: int32 [2, 16, 16], P('grp', 'col'), may hold values from 0 to 3, as said below
- block_ngrams: int32 [2, 16, 16], P('grp', 'col'), may hold values from 0 to 3, as said below
- block_counts: int32 [2, 16], P('grp', 'col'), may hold values from 4 to 16, as said below
- pmi: bfloat16 [2, 16, 16, 128, 128], P('grp', 'col'), may hold values from -6 to 6
- weights: bfloat16 [2, 16, 16, 128, 128], P('grp', 'col'), may hold values from 0.049804688 to 1
Outputs:
- doc_out: float32 [1024, 256], P(('grp', 'col'))
- ngram_out: float32 [8192, 256], P('col')
The draws below stay inside these ranges and needn't reach their ends.
Inputs may be any that keep to these rules, and one draw needn't show every extreme that they name: `block_docs`: within one device's slots every pair (document block, n-gram block) appears exactly once. `block_ngrams`: paired with block_docs as stated there. `block_counts`: some device has all 16 slots live.
All inputs are finite; a program needn't handle non-finite values.
Results may differ from the reference program's by a relative error of at most 0.0086.
Values may be sent and summed in bfloat16 or wider, within the bound.
No kernel may reach another device: no remote copies, remote signals or barrier semaphores. Data moves between devices by JAX's collectives and lax.ppermute only.
A program may use at most 64 MiB of HBM per device.

```python
import math
import jax
import jax.numpy as jnp
from jax import lax

R = 256
BLK = 128
DBG = 4
NGB = 4
CAP = 16
GROUPS = 2
SHARDS = 16
NDOC = 1024
NNG = 8192
N_GRP = 2
N_COL = 16


def pair_table(key):
    keys = jax.random.split(jax.random.fold_in(key, 7), GROUPS * SHARDS)
    orders = jax.vmap(lambda one: jax.random.permutation(one, CAP))(keys)
    return orders.reshape(GROUPS, SHARDS, CAP).astype(jnp.int32)


def draw_block_docs(key, part):
    return (pair_table(key) // NGB).astype(jnp.int32)


def draw_block_ngrams(key, part):
    return (pair_table(key) % NGB).astype(jnp.int32)


def draw_block_counts(key, part):
    spread = jax.random.randint(jax.random.fold_in(key, 11), (GROUPS * SHARDS,), 0, CAP - 3)
    counts = 4 + spread * spread // (CAP - 4)
    chosen = jax.random.randint(jax.random.fold_in(key, 12), (), 0, GROUPS * SHARDS)
    counts = counts.at[chosen].set(CAP)
    return counts.reshape(GROUPS, SHARDS).astype(jnp.int32)


def draw_doc_factors(key, part):
    first = jax.random.fold_in(key, 31)
    values = 0.25 * jax.random.normal(first, (NDOC, R), jnp.float32)
    return jnp.clip(values, -1.5, 1.5).astype(jnp.float32)


def draw_ngram_factors(key, part):
    first = jax.random.fold_in(key, 41)
    values = 0.25 * jax.random.normal(first, (NNG, R), jnp.float32)
    return jnp.clip(values, -1.5, 1.5).astype(jnp.float32)


def block_levels(own_key, extent, shards, least, high):
    gain, own = 1.0, jax.random.fold_in(own_key, 6)
    for axis_at, shards_of in shards:
        heights = jnp.exp(jax.random.uniform(jax.random.fold_in(own, axis_at), (shards_of,), jnp.float32, least / len(shards), high / len(shards)))
        gain = gain * jnp.repeat(heights, extent[axis_at] // shards_of).reshape([-1 if axis == axis_at else 1 for axis in range(len(extent))])
    return gain


def normal_values(key, dims, deviation, most, cuts=(), kind=jnp.bfloat16):
    drawn = deviation * jax.random.normal(key, dims, jnp.float32)
    if cuts:
        drawn = drawn * block_levels(key, dims, cuts, -0.22, 0.18)
    return jnp.clip(drawn, -most, most).astype(kind)


def setup_inputs(seed: int = 0) -> dict:
    key_of = jax.random.split(jax.random.key(seed), 8)
    doc_factors = draw_doc_factors(jax.random.fold_in(key_of[7], 71), 0)
    ngram_factors = draw_ngram_factors(jax.random.fold_in(key_of[7], 71), 0)
    block_docs = draw_block_docs(jax.random.fold_in(key_of[7], 71), 0)
    block_ngrams = draw_block_ngrams(jax.random.fold_in(key_of[7], 71), 0)
    block_counts = draw_block_counts(jax.random.fold_in(key_of[7], 71), 0)
    pmi = normal_values(key_of[5], (GROUPS, SHARDS, CAP, BLK, BLK), 1.0, 6.0, ((0, 2), (1, 16)))
    weights = jnp.clip(jnp.exp(math.log(1.0) - 2.9996462 * jax.random.uniform(key_of[6], (GROUPS, SHARDS, CAP, BLK, BLK), jnp.float32) ** block_levels(key_of[6], (GROUPS, SHARDS, CAP, BLK, BLK), ((0, 2), (1, 16)), -0.2, 0.2)), 0.049804688, 1.0).astype(jnp.bfloat16)
    return dict(doc_factors=doc_factors, ngram_factors=ngram_factors, block_docs=block_docs, block_ngrams=block_ngrams, block_counts=block_counts, pmi=pmi, weights=weights)


def gradients(doc_now, ngram_now, block_docs, block_ngrams, block_counts, pmi, weights):
    highest = lax.Precision.HIGHEST
    doc_half = lax.optimization_barrier(doc_now.astype(jnp.bfloat16))
    ngram_half = lax.optimization_barrier(ngram_now.astype(jnp.bfloat16))
    doc_blocks = doc_half.reshape(N_GRP * DBG, BLK, R)
    ngram_blocks = ngram_half.reshape(N_COL * NGB, BLK, R)
    slots = jnp.arange(CAP, dtype=jnp.int32)
    total = N_GRP * N_COL
    group_ids = (jnp.arange(total, dtype=jnp.int32) // N_COL).astype(jnp.int32)
    shard_ids = (jnp.arange(total, dtype=jnp.int32) % N_COL).astype(jnp.int32)

    def visit(carry, item):
        grad_doc, grad_ngram = carry
        docs, ngrams, count, tiles, scales, group, shard = item
        doc_ids = (group * DBG + docs).astype(jnp.int32)
        ngram_ids = (shard * NGB + ngrams).astype(jnp.int32)
        left = doc_blocks[doc_ids].astype(jnp.float32)
        right = ngram_blocks[ngram_ids].astype(jnp.float32)
        scores = jnp.einsum('kir,kjr->kij', left, right, precision=highest)
        live = (slots < count).astype(jnp.float32)
        err = (live[:, None, None] * scales.astype(jnp.float32) * (scores - tiles.astype(jnp.float32))).astype(jnp.bfloat16)
        err = lax.optimization_barrier(err).astype(jnp.float32)
        grad_doc = grad_doc.at[doc_ids].add(jnp.einsum('kij,kjr->kir', err, right, precision=highest))
        grad_ngram = grad_ngram.at[ngram_ids].add(jnp.einsum('kij,kir->kjr', err, left, precision=highest))
        return ((grad_doc, grad_ngram), None)
    start = (jnp.zeros((N_GRP * DBG, BLK, R), jnp.float32), jnp.zeros((N_COL * NGB, BLK, R), jnp.float32))
    items = (block_docs.reshape(total, CAP), block_ngrams.reshape(total, CAP), block_counts.reshape(total), pmi.reshape(total, CAP, BLK, BLK), weights.reshape(total, CAP, BLK, BLK), group_ids, shard_ids)
    (grad_doc, grad_ngram), unused = lax.scan(visit, start, items)
    return (grad_doc.reshape(doc_now.shape), grad_ngram.reshape(ngram_now.shape))

def reference(doc_factors, ngram_factors, block_docs, block_ngrams, block_counts, pmi, weights):
    doc_base = math.sqrt(NNG) + 1.5 * math.sqrt(R)
    ngram_base = math.sqrt(NDOC) + 1.5 * math.sqrt(R)
    doc_rate = 100.0 / (doc_base * doc_base)
    ngram_rate = 100.0 / (ngram_base * ngram_base)
    doc_now = doc_factors
    ngram_now = ngram_factors
    for step in range(2):
        grad_doc, grad_ngram = gradients(doc_now, ngram_now, block_docs, block_ngrams, block_counts, pmi, weights)
        doc_now = doc_now - doc_rate * grad_doc
        ngram_now = ngram_now - ngram_rate * grad_ngram
    return (doc_now, ngram_now)
```

```python
import functools
import math

import jax
import jax.numpy as jnp
from jax import lax
from jax.experimental import pallas as pl
from jax.experimental.pallas import tpu as pltpu
from jax.sharding import PartitionSpec as P

R = 256
BLK = 128
BF = jnp.bfloat16
F32 = jnp.float32
VMEM = pl.BlockSpec(memory_space=pltpu.VMEM)
SMEM = pl.BlockSpec(memory_space=pltpu.SMEM)


def dot(a, b, dims):
    return lax.dot_general(a, b, (dims, ((), ())), preferred_element_type=F32)


def tile_errors(chunk, place, docs, ngrams, counts, pmi, weights, s, e):
    count = counts[0, 0]
    for k in range(pmi.shape[2]):
        d = docs[0, 0, k]
        lanes = pl.ds(pl.multiple_of(ngrams[0, 0, k] * BLK, BLK), BLK)
        live = (k < count).astype(F32)
        for i in range(BLK // chunk):
            at, row = place(d, i)
            at = pl.ds(pl.multiple_of(at, chunk), chunk)
            row = pl.ds(pl.multiple_of(row, chunk), chunk)
            p = pmi[0, 0, k, row, :].astype(F32)
            w = weights[0, 0, k, row, :].astype(F32)
            e[at, lanes] = (live * w * (s[at, lanes] - p)).astype(BF)


def relative_place(me, chunk):
    low = me & 3
    z = me >> 2

    def place(d, i):
        c, x = i & 1, i >> 1
        return ((c * 2 + x) * 4 + (d ^ z)) * chunk, ((x * 2 + c) ^ low) * chunk

    return place


def first_kernel(docs, ngrams, counts, pmi, weights, quarter, other, half, v, keep, send, gv, s, e, u, v16):
    n = quarter.shape[0]
    u[:n, :] = quarter[...]
    u[n : 2 * n, :] = other[...]
    u[2 * n :, :] = half[...]
    v16[...] = v[...].astype(BF)
    gradients(docs, ngrams, counts, pmi, weights, keep, send, gv, s, e, u, v16)


def second_kernel(
    rate, docs, ngrams, counts, pmi, weights, quarter, other, half, v, gv_own, gv_other,
    keep, send, gv, v_out, s, e, u, v16,
):
    n = quarter.shape[0]
    u[:n, :] = quarter[...]
    u[n : 2 * n, :] = other[...]
    u[2 * n :, :] = half[...]
    now = v[...] - rate * (gv_own[...].astype(F32) + gv_other[...].astype(F32))
    v_out[...] = now
    v16[...] = now.astype(BF)
    gradients(docs, ngrams, counts, pmi, weights, keep, send, gv, s, e, u, v16)


def gradients(docs, ngrams, counts, pmi, weights, keep, send, gv, s, e, u, v16):
    n = keep.shape[0]
    chunk = 2 * n // 16
    s[...] = dot(u[...], v16[...], ((1,), (1,)))
    place = relative_place(lax.axis_index("col"), chunk)
    tile_errors(chunk, place, docs, ngrams, counts, pmi, weights, s, e)
    gu = dot(e[...], v16[...], ((1,), (0,)))
    keep[...] = gu[:n, :]
    send[...] = gu[n:, :].astype(BF)
    gv[...] = dot(e[...], u[...], ((0,), (0,))).astype(BF)


def step_call(kernel, rows, ngram_rows, extra_out, arrays):
    return pl.pallas_call(
        kernel,
        out_shape=[
            jax.ShapeDtypeStruct((rows // 2, R), F32),
            jax.ShapeDtypeStruct((rows // 2, R), BF),
            jax.ShapeDtypeStruct((ngram_rows, R), BF),
        ]
        + extra_out,
        in_specs=[SMEM] * 3 + [VMEM] * (len(arrays) - 3),
        out_specs=[VMEM] * (3 + len(extra_out)),
        scratch_shapes=[
            pltpu.VMEM((rows, ngram_rows), F32),
            pltpu.VMEM((rows, ngram_rows), BF),
            pltpu.VMEM((rows, R), BF),
            pltpu.VMEM((ngram_rows, R), BF),
        ],
        compiler_params=pltpu.CompilerParams(vmem_limit_bytes=24 * 1024 * 1024),
        cost_estimate=pl.CostEstimate(
            flops=6 * rows * ngram_rows * R, bytes_accessed=4 * rows * ngram_rows, transcendentals=0
        ),
    )(*arrays)


def swap(x, bit):
    return lax.ppermute(x, "col", [(i, i ^ bit) for i in range(lax.axis_size("col"))])


def swap_group(x):
    return lax.ppermute(x, "grp", [(0, 1), (1, 0)])


def spread(quarter):
    other = swap(quarter, 2)
    half = swap(jnp.concatenate([quarter, other], 0), 1)
    return other, half


def gather_quarter(own):
    far = {j: swap(own, 4 * j) for j in (3, 2, 1)}
    return jnp.concatenate([own] + [far[j] for j in (1, 2, 3)], 0)


def quarter_sum(keep, send):
    n = keep.shape[0] // 2
    got = swap(send, 1).astype(F32)
    got_x = swap((keep[n:] + got[n:]).astype(BF), 2).astype(F32)
    return keep[:n] + got[:n] + got_x


def small_slice(doc_now, ngram_now, block_docs, block_ngrams, block_counts, pmi, weights, rates):
    doc_rate, ngram_rate = rates
    own = doc_now.shape[0]
    rows = own * 16
    ngram_rows = ngram_now.shape[0]
    slots = (block_docs, block_ngrams, block_counts, pmi, weights)

    quarter = gather_quarter(doc_now.astype(BF))
    other, half = spread(quarter)
    keep, send, gv = step_call(
        first_kernel, rows, ngram_rows, [], (*slots, quarter, other, half, ngram_now)
    )
    gv_other = swap_group(gv)
    part = quarter_sum(keep, send)
    part16 = part.astype(BF)
    far = {j: swap(part16, 4 * j) for j in (3, 2, 1)}
    sums = []
    for z in range(4):
        total = part[z * own : (z + 1) * own]
        for j in (1, 2, 3):
            k = z ^ j
            total = total + far[j][k * own : (k + 1) * own].astype(F32)
        sums.append(total)
    doc_now = doc_now - doc_rate * sums[0]
    quarter = jnp.concatenate(
        [doc_now.astype(BF)]
        + [
            (quarter[z * own : (z + 1) * own].astype(F32) - doc_rate * sums[z]).astype(BF)
            for z in (1, 2, 3)
        ],
        0,
    )
    other, half = spread(quarter)
    keep, send, gv, ngram_now = step_call(
        functools.partial(second_kernel, ngram_rate),
        rows,
        ngram_rows,
        [jax.ShapeDtypeStruct((ngram_rows, R), F32)],
        (*slots, quarter, other, half, ngram_now, gv, gv_other),
    )
    gv_other = swap_group(gv)
    part = quarter_sum(keep, send)
    total = part[:own]
    for j in (3, 2, 1):
        total = total + swap(part[j * own : (j + 1) * own].astype(BF), 4 * j).astype(F32)
    doc_now = doc_now - doc_rate * total
    ngram_now = ngram_now - ngram_rate * (gv.astype(F32) + gv_other.astype(F32))
    return doc_now, ngram_now


def plain_kernel(docs, ngrams, counts, pmi, weights, u, v, gu, gv, s, e):
    v16 = v[...].astype(BF)
    s[...] = dot(u[...], v16, ((1,), (1,)))
    tile_errors(
        BLK, lambda d, i: (d * BLK, 0), docs, ngrams, counts, pmi, weights, s, e
    )
    gu[...] = dot(e[...], v16, ((1,), (0,)))
    gv[...] = dot(e[...], u[...], ((0,), (0,)))


def any_slice(doc_now, ngram_now, block_docs, block_ngrams, block_counts, pmi, weights, rates):
    doc_rate, ngram_rate = rates
    slots = (block_docs, block_ngrams, block_counts, pmi, weights)
    rows = doc_now.shape[0] * lax.axis_size("col")
    ngram_rows = ngram_now.shape[0]
    for step in range(2):
        u = lax.all_gather(doc_now.astype(BF), "col", axis=0, tiled=True)
        gu, gv = pl.pallas_call(
            plain_kernel,
            out_shape=[
                jax.ShapeDtypeStruct((rows, R), F32),
                jax.ShapeDtypeStruct((ngram_rows, R), F32),
            ],
            in_specs=[SMEM] * 3 + [VMEM] * 4,
            out_specs=[VMEM] * 2,
            scratch_shapes=[
                pltpu.VMEM((rows, ngram_rows), F32),
                pltpu.VMEM((rows, ngram_rows), BF),
            ],
            compiler_params=pltpu.CompilerParams(vmem_limit_bytes=24 * 1024 * 1024),
        )(*slots, u, ngram_now)
        doc_now = doc_now - doc_rate * lax.psum_scatter(gu, "col", scatter_dimension=0, tiled=True)
        ngram_now = ngram_now - ngram_rate * lax.psum(gv, "grp")
    return doc_now, ngram_now


def shards(doc_factors, ngram_factors, block_docs, block_ngrams, block_counts, pmi, weights):
    shard_count = lax.axis_size("col")
    group_count = lax.axis_size("grp")
    doc_total = doc_factors.shape[0] * shard_count * group_count
    ngram_total = ngram_factors.shape[0] * shard_count
    width = doc_factors.shape[1]
    doc_base = math.sqrt(ngram_total) + 1.5 * math.sqrt(width)
    ngram_base = math.sqrt(doc_total) + 1.5 * math.sqrt(width)
    rates = (100.0 / (doc_base * doc_base), 100.0 / (ngram_base * ngram_base))
    run = small_slice if (group_count, shard_count) == (2, 16) else any_slice
    return run(
        doc_factors, ngram_factors, block_docs, block_ngrams, block_counts, pmi, weights, rates
    )


def solution(mesh):
    return jax.shard_map(
        shards,
        mesh=mesh,
        in_specs=(
            P(("grp", "col"), None),
            P("col", None),
            P("grp", "col", None),
            P("grp", "col", None),
            P("grp", "col"),
            P("grp", "col", None, None, None),
            P("grp", "col", None, None, None),
        ),
        out_specs=(P(("grp", "col"), None), P("col", None)),
        check_vma=False,
    )
```

```python
import functools
import math

import jax
import jax.numpy as jnp
from jax import lax
from jax.experimental import pallas as pl
from jax.experimental.pallas import tpu as pltpu
from jax.sharding import PartitionSpec as P

R = 256
BLK = 128
BF = jnp.bfloat16
F32 = jnp.float32
VMEM = pl.BlockSpec(memory_space=pltpu.VMEM)
SMEM = pl.BlockSpec(memory_space=pltpu.SMEM)
HBM = pl.BlockSpec(memory_space=pltpu.HBM)
ANY = pl.BlockSpec(memory_space=pl.ANY)
MIB = 1024 * 1024
PLACE_VMEM = 53 * MIB
LONG = 10**11


def dot(a, b, dims):
    return lax.dot_general(a, b, (dims, ((), ())), preferred_element_type=F32)


def shape(rows, columns, dtype):
    return jax.ShapeDtypeStruct((rows, columns), dtype)


def call(kernel, outs, in_specs, arrays, scratch=(), flops=0, vmem=16 * MIB):
    read = sum(a.size * a.dtype.itemsize for a in arrays)
    return pl.pallas_call(
        kernel,
        out_shape=outs,
        in_specs=in_specs,
        out_specs=[VMEM] * len(outs),
        scratch_shapes=list(scratch),
        compiler_params=pltpu.CompilerParams(vmem_limit_bytes=vmem),
        cost_estimate=pl.CostEstimate(flops=flops, bytes_accessed=read, transcendentals=0),
    )(*arrays)


ALONG_X = 3
ALONG_Z = (0, 5, 9, 12)
OTHER_CORE = 1


def place_kernel(
    docs, ngrams, counts, pmi_hbm, weights_hbm, v_hbm, mine, theirs, v16, pmi, weights, v, sems, v_sem
):
    slots = pmi.shape[0]
    parts = sems.shape[1]
    v_copy = pltpu.make_async_copy(v_hbm, v, v_sem)
    v_copy.start()
    copies = []
    for a, (src, dst) in enumerate(((weights_hbm, weights), (pmi_hbm, pmi))):
        for i in range(parts):
            some = pl.ds(i * (slots // parts), slots // parts)
            copies.append(pltpu.make_async_copy(src.at[0, 0, some], dst.at[some], sems.at[a, i]))
            copies[-1].start()
    half = mine.shape[0] // 2
    v_half = v.shape[0] // 2
    v_copy.wait()
    now = v[...].astype(BF)
    v16[...] = now
    theirs[2 * half :, :R] = now[:v_half]
    theirs[2 * half :, R:] = now[v_half:]
    me = lax.axis_index("col")
    low, my_z = me & 3, me >> 2
    count = counts[0, 0]
    own = half // 8
    for k in range(slots):
        if k % (slots // parts) == 0:
            for a in range(2):
                copies[a * parts + k // (slots // parts)].wait()
        lanes = pl.ds(pl.multiple_of(ngrams[0, 0, k] * BLK, BLK), BLK)
        z = docs[0, 0, k] ^ my_z
        first = low ^ ((z ^ (z >> 1)) & 1)
        live = k < count
        for x in range(2):
            at = pl.multiple_of((x * 4 + z) * own, own)
            for h, out in enumerate((mine, theirs)):
                rows = pl.ds(pl.multiple_of((first ^ (x * 2) ^ (x ^ h)) * own, own), own)
                tile = weights[k, rows, :]
                out[pl.ds(at, own), lanes] = jnp.where(live, tile, jnp.zeros_like(tile))
                out[pl.ds(at + half, own), lanes] = pmi[k, rows, :]


def errors_and_gu(u, v_blocks, tiles, e):
    half = u.shape[0]
    gu = None
    for i, v in enumerate(v_blocks):
        width = v.shape[0]
        lanes = slice(i * width, (i + 1) * width)
        s = dot(u, v, ((1,), (1,)))
        w = tiles[:half, lanes].astype(F32)
        p = tiles[half : 2 * half, lanes].astype(F32)
        err = (w * (s - p)).astype(BF)
        e[:, lanes] = err
        term = dot(err, v, ((1,), (0,)))
        gu = term if gu is None else gu + term
    return gu


def pair_kernel(near, other, pair):
    own = near.shape[0]
    pair[:own, :] = near[...].astype(BF)
    pair[own:, :] = other[...].astype(BF)


def own_kernel(pair, far1, far2, far3, v16, mine, u, e, gu):
    own = pair.shape[0] // 2
    for x in range(2):
        for z, far in enumerate((pair, far1, far2, far3)):
            at = (x * 4 + z) * own
            u[at : at + own, :] = far[x * own : (x + 1) * own, :]
    n = v16.shape[0] // 2
    gu[...] = errors_and_gu(u[...], [v16[:n], v16[n:]], mine, e)


def theirs_kernel(u, gu_own, theirs, *rest):
    *v16_theirs, keep, send1, send2, send3, e = rest
    half = u.shape[0]
    own = half // 8
    if v16_theirs:
        (v16,) = v16_theirs
        n = v16.shape[0] // 2
        v_blocks = [v16[:n], v16[n:]]
    else:
        v_blocks = [theirs[2 * half :, :R], theirs[2 * half :, R:]]
    gu = gu_own[...] + errors_and_gu(u[...], v_blocks, theirs, e)
    for z, out in enumerate((keep, send1, send2, send3)):
        for x in range(2):
            at = (x * 4 + z) * own
            out[x * own : (x + 1) * own, :] = gu[at : at + own].astype(out.dtype)


def along_z_kernel(keep, got1, got2, got3, total, total16):
    now = keep[...] + got1[...].astype(F32) + got2[...].astype(F32) + got3[...].astype(F32)
    total[...] = now
    total16[...] = now.astype(BF)


def pair_update_kernel(rate, doc, pair, total, got, doc_out, pair_out):
    own = doc.shape[0]
    now = doc[...] - rate * (total[:own, :] + got[own:, :].astype(F32))
    doc_out[...] = now
    pair_out[:own, :] = now.astype(BF)
    now = pair[own:, :].astype(F32) - rate * (total[own:, :] + got[:own, :].astype(F32))
    pair_out[own:, :] = now.astype(BF)


def ngram_update_kernel(rate, ours, got, v, after, v_out, v16):
    now = v[...] - rate * (ours[...].astype(F32) + got[...].astype(F32))
    v_out[...] = now
    v16[...] = now.astype(BF)


def ngram_kernel(e, e_theirs, u, keep, send):
    send[...] = dot(e_theirs[...], u[...], ((0,), (0,))).astype(BF)
    keep[...] = dot(e[...], u[...], ((0,), (0,)))


def swap(x, mask):
    return lax.ppermute(x, "col", [(i, i ^ mask) for i in range(lax.axis_size("col"))])


def along_z(blocks):
    got = [swap(blocks[j - 1], ALONG_Z[j]) for j in (3, 2, 1)]
    return got[::-1]


def swap_group(x):
    return lax.ppermute(x, "grp", [(0, 1), (1, 0)])


def small_slice(doc_now, ngram_now, block_docs, block_ngrams, block_counts, pmi, weights, rates):
    doc_rate, ngram_rate = rates
    own = doc_now.shape[0]
    half = 8 * own
    n = ngram_now.shape[0]
    slots = pmi.shape[2]
    flops = 2 * 2 * half * 2 * n * R
    ngram_grads = [shape(n, R, F32), shape(n, R, BF)]

    other = swap(doc_now, ALONG_X)
    mine, theirs, v16 = call(
        place_kernel,
        [shape(2 * half, n, BF), shape(3 * half, n, BF), shape(n, R, BF)],
        [SMEM] * 3 + [HBM] * 3,
        (block_docs, block_ngrams, block_counts, pmi, weights, ngram_now),
        [
            pltpu.VMEM((slots, BLK, BLK), BF),
            pltpu.VMEM((slots, BLK, BLK), BF),
            pltpu.VMEM((n, R), F32),
            pltpu.SemaphoreType.DMA((2, 4)),
            pltpu.SemaphoreType.DMA,
        ],
        vmem=PLACE_VMEM,
    )
    theirs, other = lax.optimization_barrier((theirs, other))
    (pair,) = call(pair_kernel, [shape(2 * own, R, BF)], [VMEM] * 2, (doc_now, other))
    far = along_z([pair] * 3)
    theirs = swap(theirs, OTHER_CORE)
    def gradients(pair, far, v16, *v16_theirs):
        u, e, gu = call(
            own_kernel,
            [shape(half, R, BF), shape(half, n, BF), shape(half, R, F32)],
            [VMEM] * 6,
            (pair, *far, v16, mine),
            flops=LONG,
        )
        keep, *send, e_theirs = call(
            theirs_kernel,
            [shape(2 * own, R, F32)] + [shape(2 * own, R, BF)] * 3 + [shape(half, n, BF)],
            [VMEM] * (3 + len(v16_theirs)),
            (u, gu, theirs, *v16_theirs),
            flops=flops // 2,
        )
        got = along_z(send)
        gv_keep, gv_send = call(
            ngram_kernel, ngram_grads, [VMEM] * 3, (e, e_theirs, u), flops=flops // 2
        )
        ours = (gv_keep + swap(gv_send, OTHER_CORE).astype(F32)).astype(BF)
        return keep, got, ours, swap_group(ours)

    keep, got, ours, ngram_got = gradients(pair, far, v16)
    total, total16 = call(
        along_z_kernel,
        [shape(2 * own, R, F32), shape(2 * own, R, BF)],
        [VMEM] * 4,
        (keep, *got),
        flops=LONG,
    )
    doc_now, pair = call(
        functools.partial(pair_update_kernel, doc_rate),
        [shape(own, R, F32), shape(2 * own, R, BF)],
        [VMEM] * 4,
        (doc_now, pair, total, swap(total16, ALONG_X)),
        flops=LONG,
    )
    far = along_z([pair] * 3)
    ngram_now, v16 = call(
        functools.partial(ngram_update_kernel, ngram_rate),
        [shape(n, R, F32), shape(n, R, BF)],
        [VMEM] * 3 + [ANY],
        (ours, ngram_got, ngram_now, pair),
    )
    v16_theirs = swap(v16, OTHER_CORE)

    keep, got, ours, ngram_got = gradients(pair, far, v16, v16_theirs)
    for some in got:
        keep = keep + some.astype(F32)
    total = keep[:own] + swap(keep[own:].astype(BF), ALONG_X).astype(F32)
    ngram_now = ngram_now - ngram_rate * (ours.astype(F32) + ngram_got.astype(F32))
    doc_now = doc_now - doc_rate * total
    return doc_now, ngram_now


def plain_kernel(docs, ngrams, counts, pmi, weights, u, v, gu, gv, s, e):
    v16 = v[...].astype(BF)
    s[...] = dot(u[...], v16, ((1,), (1,)))
    count = counts[0, 0]
    for k in range(pmi.shape[2]):
        rows = pl.ds(pl.multiple_of(docs[0, 0, k] * BLK, BLK), BLK)
        lanes = pl.ds(pl.multiple_of(ngrams[0, 0, k] * BLK, BLK), BLK)
        live = (k < count).astype(F32)
        p = pmi[0, 0, k].astype(F32)
        w = weights[0, 0, k].astype(F32)
        e[rows, lanes] = (live * w * (s[rows, lanes] - p)).astype(BF)
    gu[...] = dot(e[...], v16, ((1,), (0,)))
    gv[...] = dot(e[...], u[...], ((0,), (0,)))


def any_slice(doc_now, ngram_now, block_docs, block_ngrams, block_counts, pmi, weights, rates):
    doc_rate, ngram_rate = rates
    slots = (block_docs, block_ngrams, block_counts, pmi, weights)
    rows = doc_now.shape[0] * lax.axis_size("col")
    n = ngram_now.shape[0]
    for step in range(2):
        u = lax.all_gather(doc_now.astype(BF), "col", axis=0, tiled=True)
        gu, gv = call(
            plain_kernel,
            [shape(rows, R, F32), shape(n, R, F32)],
            [SMEM] * 3 + [VMEM] * 4,
            (*slots, u, ngram_now),
            [pltpu.VMEM((rows, n), F32), pltpu.VMEM((rows, n), BF)],
            flops=6 * rows * n * R,
        )
        doc_now = doc_now - doc_rate * lax.psum_scatter(gu, "col", scatter_dimension=0, tiled=True)
        ngram_now = ngram_now - ngram_rate * lax.psum(gv, "grp")
    return doc_now, ngram_now


def shards(doc_factors, ngram_factors, block_docs, block_ngrams, block_counts, pmi, weights):
    shard_count = lax.axis_size("col")
    group_count = lax.axis_size("grp")
    doc_total = doc_factors.shape[0] * shard_count * group_count
    ngram_total = ngram_factors.shape[0] * shard_count
    width = doc_factors.shape[1]
    doc_base = math.sqrt(ngram_total) + 1.5 * math.sqrt(width)
    ngram_base = math.sqrt(doc_total) + 1.5 * math.sqrt(width)
    rates = (100.0 / (doc_base * doc_base), 100.0 / (ngram_base * ngram_base))
    run = small_slice if (group_count, shard_count) == (2, 16) else any_slice
    return run(
        doc_factors, ngram_factors, block_docs, block_ngrams, block_counts, pmi, weights, rates
    )


def solution(mesh):
    return jax.shard_map(
        shards,
        mesh=mesh,
        in_specs=(
            P(("grp", "col"), None),
            P("col", None),
            P("grp", "col", None),
            P("grp", "col", None),
            P("grp", "col"),
            P("grp", "col", None, None, None),
            P("grp", "col", None, None, None),
        ),
        out_specs=(P(("grp", "col"), None), P("col", None)),
        check_vma=False,
    )
```

```python
import functools
import math

import jax
import jax.numpy as jnp
from jax import lax
from jax.experimental import pallas as pl
from jax.experimental.pallas import tpu as pltpu
from jax.sharding import PartitionSpec as P

R = 256
BLK = 128
BF = jnp.bfloat16
F32 = jnp.float32
VMEM = pl.BlockSpec(memory_space=pltpu.VMEM)
SMEM = pl.BlockSpec(memory_space=pltpu.SMEM)
HBM = pl.BlockSpec(memory_space=pltpu.HBM)
ANY = pl.BlockSpec(memory_space=pl.ANY)
MIB = 1024 * 1024
PLACE_VMEM = int(52.4 * MIB)
LONG = 10**11


def dot(a, b, dims):
    return lax.dot_general(a, b, (dims, ((), ())), preferred_element_type=F32)


def shape(rows, columns, dtype):
    return jax.ShapeDtypeStruct((rows, columns), dtype)


def call(kernel, outs, in_specs, arrays, scratch=(), flops=0, read=None, vmem=16 * MIB):
    if read is None:
        read = sum(a.size * a.dtype.itemsize for a in arrays)
    return pl.pallas_call(
        kernel,
        out_shape=outs,
        in_specs=in_specs,
        out_specs=[VMEM] * len(outs),
        scratch_shapes=list(scratch),
        compiler_params=pltpu.CompilerParams(vmem_limit_bytes=vmem),
        cost_estimate=pl.CostEstimate(flops=flops, bytes_accessed=read, transcendentals=0),
    )(*arrays)


FAR = 9
NEAR = (0, 3, 5, 7)
OTHER_CORE = 1


def place_kernel(
    docs, ngrams, counts, pmi_hbm, weights_hbm, v_hbm, mine, theirs, v16, pmi, weights, v, sems, v_sem
):
    slots = pmi.shape[0]
    parts = sems.shape[1]
    v_copy = pltpu.make_async_copy(v_hbm, v, v_sem)
    v_copy.start()
    copies = []
    for a, (src, dst) in enumerate(((weights_hbm, weights), (pmi_hbm, pmi))):
        for i in range(parts):
            some = pl.ds(i * (slots // parts), slots // parts)
            copies.append(pltpu.make_async_copy(src.at[0, 0, some], dst.at[some], sems.at[a, i]))
            copies[-1].start()
    half = mine.shape[0] // 2
    me = lax.axis_index("col")
    low, my_z = me & 3, me >> 2
    count = counts[0, 0]
    own = half // 8
    for k in range(slots):
        if k % (slots // parts) == 0:
            for a in range(2):
                copies[a * parts + k // (slots // parts)].wait()
        lanes = pl.ds(pl.multiple_of(ngrams[0, 0, k] * BLK, BLK), BLK)
        z = docs[0, 0, k] ^ my_z
        near, far = z & 1, z >> 1
        live = k < count
        for x in range(2):
            at = pl.multiple_of((far * 4 + near * 2 + x) * own, own)
            core = far ^ (near | x)
            for h, out in enumerate((mine, theirs)):
                rows = pl.ds(pl.multiple_of((low ^ (x * 2 + h) ^ core) * own, own), own)
                tile = weights[k, rows, :]
                out[pl.ds(at, own), lanes] = jnp.where(live, tile, jnp.zeros_like(tile))
                out[pl.ds(at + half, own), lanes] = pmi[k, rows, :]
    v_copy.wait()
    v16[...] = v[...].astype(BF)


def errors_and_gu(u, v_blocks, tiles, e):
    half = u.shape[0]
    gu = None
    for i, v in enumerate(v_blocks):
        width = v.shape[0]
        lanes = slice(i * width, (i + 1) * width)
        s = dot(u, v, ((1,), (1,)))
        w = tiles[:half, lanes].astype(F32)
        p = tiles[half : 2 * half, lanes].astype(F32)
        err = (w * (s - p)).astype(BF)
        e[:, lanes] = err
        term = dot(err, v, ((1,), (0,)))
        gu = term if gu is None else gu + term
    return gu


def pair_kernel(near, other, pair):
    own = near.shape[0]
    pair[:own, :] = near[...].astype(BF)
    pair[own:, :] = other[...].astype(BF)


def rows_kernel(pair, far1, far2, far3, u):
    own = pair.shape[0] // 2
    for x in range(2):
        for z, far in enumerate((pair, far1, far2, far3)):
            at = (x * 4 + z) * own
            u[at : at + own, :] = far[x * own : (x + 1) * own, :]


def all_gu(u, v16, v16_theirs, mine, theirs, e, e_theirs):
    n = v16.shape[0] // 2
    gu = errors_and_gu(u[...], [v16[:n], v16[n:]], mine, e)
    return gu + errors_and_gu(u[...], [v16_theirs[:n], v16_theirs[n:]], theirs, e_theirs)


def near_first_kernel(u, v16, v16_theirs, mine, theirs, keep, send1, send2, send3, e, e_theirs):
    own = u.shape[0] // 8
    gu = all_gu(u, v16, v16_theirs, mine, theirs, e, e_theirs)
    for z, out in enumerate((keep, send1, send2, send3)):
        for x in range(2):
            at = (x * 4 + z) * own
            out[x * own : (x + 1) * own, :] = gu[at : at + own].astype(out.dtype)


def far_first_kernel(u, v16, v16_theirs, mine, theirs, keep, send, e, e_theirs):
    n = keep.shape[0]
    gu = all_gu(u, v16, v16_theirs, mine, theirs, e, e_theirs)
    keep[...] = gu[:n]
    send[...] = gu[n:].astype(BF)


def ngram_send_kernel(e_theirs, u, send):
    send[...] = dot(e_theirs[...], u[...], ((0,), (0,))).astype(BF)


def ngram_keep_kernel(e, u, got, ours):
    ours[...] = (dot(e[...], u[...], ((0,), (0,))) + got[...].astype(F32)).astype(BF)


def near_sum_kernel(keep, got1, got2, got3, total, total16):
    now = keep[...] + got1[...].astype(F32) + got2[...].astype(F32) + got3[...].astype(F32)
    total[...] = now
    total16[...] = now.astype(BF)


def far_sum_kernel(keep, got, total, send1, send2, send3):
    own = total.shape[0]
    now = keep[...] + got[...].astype(F32)
    for j, out in enumerate((total, send1, send2, send3)):
        out[...] = now[j * own : (j + 1) * own].astype(out.dtype)


def last_kernel(
    doc_rate, ngram_rate, doc, total, got1, got2, got3, ours, ngram_got, v, doc_out, v_out
):
    v_out[...] = v[...] - ngram_rate * (ours[...].astype(F32) + ngram_got[...].astype(F32))
    now = total[...] + got1[...].astype(F32) + got2[...].astype(F32) + got3[...].astype(F32)
    doc_out[...] = doc[...] - doc_rate * now


def pair_update_kernel(rate, doc, pair, total, got, doc_out, pair_out):
    own = doc.shape[0]
    now = doc[...] - rate * (total[:own, :] + got[own:, :].astype(F32))
    doc_out[...] = now
    pair_out[:own, :] = now.astype(BF)
    now = pair[own:, :].astype(F32) - rate * (total[own:, :] + got[:own, :].astype(F32))
    pair_out[own:, :] = now.astype(BF)


def ngram_update_kernel(rate, ours, got, v, after, v_out, v16):
    now = v[...] - rate * (ours[...].astype(F32) + got[...].astype(F32))
    v_out[...] = now
    v16[...] = now.astype(BF)


def swap(x, mask):
    return lax.ppermute(x, "col", [(i, i ^ mask) for i in range(lax.axis_size("col"))])


def exchange_near(blocks):
    got = [swap(blocks[j - 1], NEAR[j]) for j in (3, 2, 1)]
    return got[::-1]


def swap_group(x):
    return lax.ppermute(x, "grp", [(0, 1), (1, 0)])


def small_slice(doc_now, ngram_now, block_docs, block_ngrams, block_counts, pmi, weights, rates):
    doc_rate, ngram_rate = rates
    own = doc_now.shape[0]
    half = 8 * own
    n = ngram_now.shape[0]
    slots = pmi.shape[2]
    flops = 2 * 2 * half * 2 * n * R

    other = swap(doc_now, FAR)
    mine, theirs, v16 = call(
        place_kernel,
        [shape(2 * half, n, BF), shape(2 * half, n, BF), shape(n, R, BF)],
        [SMEM] * 3 + [HBM] * 3,
        (block_docs, block_ngrams, block_counts, pmi, weights, ngram_now),
        [
            pltpu.VMEM((slots, BLK, BLK), BF),
            pltpu.VMEM((slots, BLK, BLK), BF),
            pltpu.VMEM((n, R), F32),
            pltpu.SemaphoreType.DMA((2, 4)),
            pltpu.SemaphoreType.DMA,
        ],
        vmem=PLACE_VMEM,
    )
    theirs, other = lax.optimization_barrier((theirs, other))
    (pair,) = call(pair_kernel, [shape(2 * own, R, BF)], [VMEM] * 2, (doc_now, other))
    far = exchange_near([pair] * 3)
    theirs = swap(theirs, OTHER_CORE)
    v16_theirs = swap(v16, OTHER_CORE)
    def gradients(kernel, keep_and_send, pair, far, v16, v16_theirs):
        (u,) = call(rows_kernel, [shape(half, R, BF)], [VMEM] * 4, (pair, *far), flops=LONG)
        *outs, e, e_theirs = call(
            kernel,
            keep_and_send + [shape(half, n, BF)] * 2,
            [VMEM] * 5,
            (u, v16, v16_theirs, mine, theirs),
            flops=flops,
        )
        (gv,) = call(
            ngram_send_kernel, [shape(n, R, BF)], [VMEM] * 2, (e_theirs, u), flops=flops // 4
        )
        (ours,) = call(
            ngram_keep_kernel,
            [shape(n, R, BF)],
            [VMEM] * 3,
            (e, u, swap(gv, OTHER_CORE)),
            flops=flops // 4,
        )
        return *outs, ours, swap_group(ours)

    keep, *send, ours, ngram_got = gradients(
        near_first_kernel,
        [shape(2 * own, R, F32)] + [shape(2 * own, R, BF)] * 3,
        pair,
        far,
        v16,
        v16_theirs,
    )
    got = exchange_near(send)
    total, total16 = call(
        near_sum_kernel,
        [shape(2 * own, R, F32), shape(2 * own, R, BF)],
        [VMEM] * 4,
        (keep, *got),
        flops=LONG,
    )
    doc_now, pair = call(
        functools.partial(pair_update_kernel, doc_rate),
        [shape(own, R, F32), shape(2 * own, R, BF)],
        [VMEM] * 4,
        (doc_now, pair, total, swap(total16, FAR)),
    )
    far = exchange_near([pair] * 3)
    ngram_now, v16 = call(
        functools.partial(ngram_update_kernel, ngram_rate),
        [shape(n, R, F32), shape(n, R, BF)],
        [VMEM] * 3 + [ANY],
        (ours, ngram_got, ngram_now, pair),
    )
    v16_theirs = swap(v16, OTHER_CORE)

    keep, send, ours, ngram_got = gradients(
        far_first_kernel,
        [shape(half // 2, R, F32), shape(half // 2, R, BF)],
        pair,
        far,
        v16,
        v16_theirs,
    )
    total, *send = call(
        far_sum_kernel,
        [shape(own, R, F32)] + [shape(own, R, BF)] * 3,
        [VMEM] * 2,
        (keep, swap(send, FAR)),
        flops=LONG,
    )
    return call(
        functools.partial(last_kernel, doc_rate, ngram_rate),
        [shape(own, R, F32), shape(n, R, F32)],
        [VMEM] * 8,
        (doc_now, total, *exchange_near(send), ours, ngram_got, ngram_now),
        read=0,
    )


def plain_kernel(docs, ngrams, counts, pmi, weights, u, v, gu, gv, s, e):
    v16 = v[...].astype(BF)
    s[...] = dot(u[...], v16, ((1,), (1,)))
    count = counts[0, 0]
    for k in range(pmi.shape[2]):
        rows = pl.ds(pl.multiple_of(docs[0, 0, k] * BLK, BLK), BLK)
        lanes = pl.ds(pl.multiple_of(ngrams[0, 0, k] * BLK, BLK), BLK)
        live = (k < count).astype(F32)
        p = pmi[0, 0, k].astype(F32)
        w = weights[0, 0, k].astype(F32)
        e[rows, lanes] = (live * w * (s[rows, lanes] - p)).astype(BF)
    gu[...] = dot(e[...], v16, ((1,), (0,)))
    gv[...] = dot(e[...], u[...], ((0,), (0,)))


def any_slice(doc_now, ngram_now, block_docs, block_ngrams, block_counts, pmi, weights, rates):
    doc_rate, ngram_rate = rates
    slots = (block_docs, block_ngrams, block_counts, pmi, weights)
    rows = doc_now.shape[0] * lax.axis_size("col")
    n = ngram_now.shape[0]
    for step in range(2):
        u = lax.all_gather(doc_now.astype(BF), "col", axis=0, tiled=True)
        gu, gv = call(
            plain_kernel,
            [shape(rows, R, F32), shape(n, R, F32)],
            [SMEM] * 3 + [VMEM] * 4,
            (*slots, u, ngram_now),
            [pltpu.VMEM((rows, n), F32), pltpu.VMEM((rows, n), BF)],
            flops=6 * rows * n * R,
        )
        doc_now = doc_now - doc_rate * lax.psum_scatter(gu, "col", scatter_dimension=0, tiled=True)
        ngram_now = ngram_now - ngram_rate * lax.psum(gv, "grp")
    return doc_now, ngram_now


def shards(doc_factors, ngram_factors, block_docs, block_ngrams, block_counts, pmi, weights):
    shard_count = lax.axis_size("col")
    group_count = lax.axis_size("grp")
    doc_total = doc_factors.shape[0] * shard_count * group_count
    ngram_total = ngram_factors.shape[0] * shard_count
    width = doc_factors.shape[1]
    doc_base = math.sqrt(ngram_total) + 1.5 * math.sqrt(width)
    ngram_base = math.sqrt(doc_total) + 1.5 * math.sqrt(width)
    rates = (100.0 / (doc_base * doc_base), 100.0 / (ngram_base * ngram_base))
    run = small_slice if (group_count, shard_count) == (2, 16) else any_slice
    return run(
        doc_factors, ngram_factors, block_docs, block_ngrams, block_counts, pmi, weights, rates
    )


def solution(mesh):
    return jax.shard_map(
        shards,
        mesh=mesh,
        in_specs=(
            P(("grp", "col"), None),
            P("col", None),
            P("grp", "col", None),
            P("grp", "col", None),
            P("grp", "col"),
            P("grp", "col", None, None, None),
            P("grp", "col", None, None, None),
        ),
        out_specs=(P(("grp", "col"), None), P("col", None)),
        check_vma=False,
    )
```

```python
import functools
import math

import jax
import jax.numpy as jnp
from jax import lax
from jax.experimental import pallas as pl
from jax.experimental.pallas import tpu as pltpu
from jax.sharding import PartitionSpec as P

R = 256
BLK = 128
BF = jnp.bfloat16
F32 = jnp.float32
VMEM = pl.BlockSpec(memory_space=pltpu.VMEM)
SMEM = pl.BlockSpec(memory_space=pltpu.SMEM)
HBM = pl.BlockSpec(memory_space=pltpu.HBM)
ANY = pl.BlockSpec(memory_space=pl.ANY)
MIB = 1024 * 1024
PLACE_VMEM = int(52.4 * MIB)
LONG = 10**11


def dot(a, b, dims):
    return lax.dot_general(a, b, (dims, ((), ())), preferred_element_type=F32)


def shape(rows, columns, dtype):
    return jax.ShapeDtypeStruct((rows, columns), dtype)


def call(kernel, outs, in_specs, arrays, scratch=(), flops=0, read=None, vmem=16 * MIB):
    if read is None:
        read = sum(a.size * a.dtype.itemsize for a in arrays)
    return pl.pallas_call(
        kernel,
        out_shape=outs,
        in_specs=in_specs,
        out_specs=[VMEM] * len(outs),
        scratch_shapes=list(scratch),
        compiler_params=pltpu.CompilerParams(vmem_limit_bytes=vmem),
        cost_estimate=pl.CostEstimate(flops=flops, bytes_accessed=read, transcendentals=0),
    )(*arrays)


FAR = 9
NEAR = (0, 3, 5, 7)
OTHER_CORE = 1


def place_kernel(
    docs, ngrams, counts, pmi_hbm, weights_hbm, v_hbm, mine, theirs, v16, pmi, weights, v, sems, v_sem
):
    slots = pmi.shape[0]
    parts = sems.shape[1]
    v_copy = pltpu.make_async_copy(v_hbm, v, v_sem)
    v_copy.start()
    copies = []
    for a, (src, dst) in enumerate(((weights_hbm, weights), (pmi_hbm, pmi))):
        for i in range(parts):
            some = pl.ds(i * (slots // parts), slots // parts)
            copies.append(pltpu.make_async_copy(src.at[0, 0, some], dst.at[some], sems.at[a, i]))
            copies[-1].start()
    half = mine.shape[0] // 2
    me = lax.axis_index("col")
    low, my_z = me & 3, me >> 2
    count = counts[0, 0]
    own = half // 8
    for k in range(slots):
        if k % (slots // parts) == 0:
            for a in range(2):
                copies[a * parts + k // (slots // parts)].wait()
        lanes = pl.ds(pl.multiple_of(ngrams[0, 0, k] * BLK, BLK), BLK)
        z = docs[0, 0, k] ^ my_z
        near, far = z & 1, z >> 1
        live = k < count
        for x in range(2):
            at = pl.multiple_of((far * 4 + near * 2 + x) * own, own)
            core = far ^ (near | x)
            for h, out in enumerate((mine, theirs)):
                rows = pl.ds(pl.multiple_of((low ^ (x * 2 + h) ^ core) * own, own), own)
                tile = weights[k, rows, :]
                out[pl.ds(at, own), lanes] = jnp.where(live, tile, jnp.zeros_like(tile))
                out[pl.ds(at + half, own), lanes] = pmi[k, rows, :]
    v_copy.wait()
    v16[...] = v[...].astype(BF)


def errors_and_gu(u, v_blocks, tiles, e):
    half = u.shape[0]
    gu = None
    for i, v in enumerate(v_blocks):
        width = v.shape[0]
        lanes = slice(i * width, (i + 1) * width)
        s = dot(u, v, ((1,), (1,)))
        w = tiles[:half, lanes].astype(F32)
        p = tiles[half : 2 * half, lanes].astype(F32)
        err = (w * (s - p)).astype(BF)
        e[:, lanes] = err
        term = dot(err, v, ((1,), (0,)))
        gu = term if gu is None else gu + term
    return gu


def pair_kernel(near, other, pair):
    own = near.shape[0]
    pair[:own, :] = near[...].astype(BF)
    pair[own:, :] = other[...].astype(BF)


def rows_kernel(pair, far1, far2, far3, u):
    own = pair.shape[0] // 2
    for x in range(2):
        for z, far in enumerate((pair, far1, far2, far3)):
            at = (x * 4 + z) * own
            u[at : at + own, :] = far[x * own : (x + 1) * own, :]


def all_gu(u, v16, v16_theirs, mine, theirs, e, gv_send, e_theirs):
    n = v16.shape[0] // 2
    gu = errors_and_gu(u[...], [v16[:n], v16[n:]], mine, e)
    gu = gu + errors_and_gu(u[...], [v16_theirs[:n], v16_theirs[n:]], theirs, e_theirs)
    gv_send[...] = dot(e_theirs[...], u[...], ((0,), (0,))).astype(BF)
    return gu


def near_first_kernel(u, *refs):
    *tiles, keep, send1, send2, send3, e, gv_send, e_theirs = refs
    own = u.shape[0] // 8
    gu = all_gu(u, *tiles, e, gv_send, e_theirs)
    for z, out in enumerate((keep, send1, send2, send3)):
        for x in range(2):
            at = (x * 4 + z) * own
            out[x * own : (x + 1) * own, :] = gu[at : at + own].astype(out.dtype)


def far_first_kernel(u, *refs):
    *tiles, keep, send, e, gv_send, e_theirs = refs
    n = keep.shape[0]
    gu = all_gu(u, *tiles, e, gv_send, e_theirs)
    keep[...] = gu[:n]
    send[...] = gu[n:].astype(BF)


def ngram_keep_kernel(e, u, got, ours):
    ours[...] = (dot(e[...], u[...], ((0,), (0,))) + got[...].astype(F32)).astype(BF)


def near_sum_kernel(keep, got1, got2, got3, total, total16):
    now = keep[...] + got1[...].astype(F32) + got2[...].astype(F32) + got3[...].astype(F32)
    total[...] = now
    total16[...] = now.astype(BF)


def far_sum_kernel(keep, got, total, send1, send2, send3):
    own = total.shape[0]
    now = keep[...] + got[...].astype(F32)
    for j, out in enumerate((total, send1, send2, send3)):
        out[...] = now[j * own : (j + 1) * own].astype(out.dtype)


def last_kernel(
    doc_rate, ngram_rate, doc, total, got1, got2, got3, ours, ngram_got, v, doc_out, v_out
):
    v_out[...] = v[...] - ngram_rate * (ours[...].astype(F32) + ngram_got[...].astype(F32))
    now = total[...] + got1[...].astype(F32) + got2[...].astype(F32) + got3[...].astype(F32)
    doc_out[...] = doc[...] - doc_rate * now


def pair_update_kernel(rate, doc, pair, total, got, doc_out, pair_out):
    own = doc.shape[0]
    now = doc[...] - rate * (total[:own, :] + got[own:, :].astype(F32))
    doc_out[...] = now
    pair_out[:own, :] = now.astype(BF)
    now = pair[own:, :].astype(F32) - rate * (total[own:, :] + got[:own, :].astype(F32))
    pair_out[own:, :] = now.astype(BF)


def ngram_update_kernel(rate, ours, got, v, after, v_out, v16):
    now = v[...] - rate * (ours[...].astype(F32) + got[...].astype(F32))
    v_out[...] = now
    v16[...] = now.astype(BF)


def swap(x, mask):
    return lax.ppermute(x, "col", [(i, i ^ mask) for i in range(lax.axis_size("col"))])


def exchange_near(blocks):
    got = [swap(blocks[j - 1], NEAR[j]) for j in (3, 2, 1)]
    return got[::-1]


def swap_group(x):
    return lax.ppermute(x, "grp", [(0, 1), (1, 0)])


def small_slice(doc_now, ngram_now, block_docs, block_ngrams, block_counts, pmi, weights, rates):
    doc_rate, ngram_rate = rates
    own = doc_now.shape[0]
    half = 8 * own
    n = ngram_now.shape[0]
    slots = pmi.shape[2]
    flops = 2 * 2 * half * 2 * n * R

    other = swap(doc_now, FAR)
    mine, theirs, v16 = call(
        place_kernel,
        [shape(2 * half, n, BF), shape(2 * half, n, BF), shape(n, R, BF)],
        [SMEM] * 3 + [HBM] * 3,
        (block_docs, block_ngrams, block_counts, pmi, weights, ngram_now),
        [
            pltpu.VMEM((slots, BLK, BLK), BF),
            pltpu.VMEM((slots, BLK, BLK), BF),
            pltpu.VMEM((n, R), F32),
            pltpu.SemaphoreType.DMA((2, 4)),
            pltpu.SemaphoreType.DMA,
        ],
        vmem=PLACE_VMEM,
    )
    theirs, other = lax.optimization_barrier((theirs, other))
    (pair,) = call(pair_kernel, [shape(2 * own, R, BF)], [VMEM] * 2, (doc_now, other))
    far = exchange_near([pair] * 3)
    theirs = swap(theirs, OTHER_CORE)
    v16_theirs = swap(v16, OTHER_CORE)
    def gradients(kernel, keep_and_send, pair, far, v16, v16_theirs):
        (u,) = call(rows_kernel, [shape(half, R, BF)], [VMEM] * 4, (pair, *far), flops=LONG)
        *outs, e, gv = call(
            kernel,
            keep_and_send + [shape(half, n, BF), shape(n, R, BF)],
            [VMEM] * 5,
            (u, v16, v16_theirs, mine, theirs),
            [pltpu.VMEM((half, n), BF)],
            flops=flops,
        )
        (ours,) = call(
            ngram_keep_kernel,
            [shape(n, R, BF)],
            [VMEM] * 3,
            (e, u, swap(gv, OTHER_CORE)),
            flops=flops // 4,
        )
        return *outs, ours, swap_group(ours)

    keep, *send, ours, ngram_got = gradients(
        near_first_kernel,
        [shape(2 * own, R, F32)] + [shape(2 * own, R, BF)] * 3,
        pair,
        far,
        v16,
        v16_theirs,
    )
    got = exchange_near(send)
    total, total16 = call(
        near_sum_kernel,
        [shape(2 * own, R, F32), shape(2 * own, R, BF)],
        [VMEM] * 4,
        (keep, *got[::-1]),
        flops=LONG,
    )
    doc_now, pair = call(
        functools.partial(pair_update_kernel, doc_rate),
        [shape(own, R, F32), shape(2 * own, R, BF)],
        [VMEM] * 4,
        (doc_now, pair, total, swap(total16, FAR)),
    )
    far = exchange_near([pair] * 3)
    ngram_now, v16 = call(
        functools.partial(ngram_update_kernel, ngram_rate),
        [shape(n, R, F32), shape(n, R, BF)],
        [VMEM] * 3 + [ANY],
        (ours, ngram_got, ngram_now, pair),
    )
    v16_theirs = swap(v16, OTHER_CORE)

    keep, send, ours, ngram_got = gradients(
        far_first_kernel,
        [shape(half // 2, R, F32), shape(half // 2, R, BF)],
        pair,
        far,
        v16,
        v16_theirs,
    )
    total, *send = call(
        far_sum_kernel,
        [shape(own, R, F32)] + [shape(own, R, BF)] * 3,
        [VMEM] * 2,
        (keep, swap(send, FAR)),
        flops=LONG,
    )
    return call(
        functools.partial(last_kernel, doc_rate, ngram_rate),
        [shape(own, R, F32), shape(n, R, F32)],
        [VMEM] * 8,
        (doc_now, total, *exchange_near(send)[::-1], ours, ngram_got, ngram_now),
        read=0,
    )


def plain_kernel(docs, ngrams, counts, pmi, weights, u, v, gu, gv, s, e):
    v16 = v[...].astype(BF)
    s[...] = dot(u[...], v16, ((1,), (1,)))
    count = counts[0, 0]
    for k in range(pmi.shape[2]):
        rows = pl.ds(pl.multiple_of(docs[0, 0, k] * BLK, BLK), BLK)
        lanes = pl.ds(pl.multiple_of(ngrams[0, 0, k] * BLK, BLK), BLK)
        live = (k < count).astype(F32)
        p = pmi[0, 0, k].astype(F32)
        w = weights[0, 0, k].astype(F32)
        e[rows, lanes] = (live * w * (s[rows, lanes] - p)).astype(BF)
    gu[...] = dot(e[...], v16, ((1,), (0,)))
    gv[...] = dot(e[...], u[...], ((0,), (0,)))


def any_slice(doc_now, ngram_now, block_docs, block_ngrams, block_counts, pmi, weights, rates):
    doc_rate, ngram_rate = rates
    slots = (block_docs, block_ngrams, block_counts, pmi, weights)
    rows = doc_now.shape[0] * lax.axis_size("col")
    n = ngram_now.shape[0]
    for step in range(2):
        u = lax.all_gather(doc_now.astype(BF), "col", axis=0, tiled=True)
        gu, gv = call(
            plain_kernel,
            [shape(rows, R, F32), shape(n, R, F32)],
            [SMEM] * 3 + [VMEM] * 4,
            (*slots, u, ngram_now),
            [pltpu.VMEM((rows, n), F32), pltpu.VMEM((rows, n), BF)],
            flops=6 * rows * n * R,
        )
        doc_now = doc_now - doc_rate * lax.psum_scatter(gu, "col", scatter_dimension=0, tiled=True)
        ngram_now = ngram_now - ngram_rate * lax.psum(gv, "grp")
    return doc_now, ngram_now


def shards(doc_factors, ngram_factors, block_docs, block_ngrams, block_counts, pmi, weights):
    shard_count = lax.axis_size("col")
    group_count = lax.axis_size("grp")
    doc_total = doc_factors.shape[0] * shard_count * group_count
    ngram_total = ngram_factors.shape[0] * shard_count
    width = doc_factors.shape[1]
    doc_base = math.sqrt(ngram_total) + 1.5 * math.sqrt(width)
    ngram_base = math.sqrt(doc_total) + 1.5 * math.sqrt(width)
    rates = (100.0 / (doc_base * doc_base), 100.0 / (ngram_base * ngram_base))
    run = small_slice if (group_count, shard_count) == (2, 16) else any_slice
    return run(
        doc_factors, ngram_factors, block_docs, block_ngrams, block_counts, pmi, weights, rates
    )


def solution(mesh):
    return jax.shard_map(
        shards,
        mesh=mesh,
        in_specs=(
            P(("grp", "col"), None),
            P("col", None),
            P("grp", "col", None),
            P("grp", "col", None),
            P("grp", "col"),
            P("grp", "col", None, None, None),
            P("grp", "col", None, None, None),
        ),
        out_specs=(P(("grp", "col"), None), P("col", None)),
        check_vma=False,
    )
```

```python
import functools
import math

import jax
import jax.numpy as jnp
from jax import lax
from jax.experimental import pallas as pl
from jax.experimental.pallas import tpu as pltpu
from jax.sharding import PartitionSpec as P

R = 256
BLK = 128
BF = jnp.bfloat16
F32 = jnp.float32
VMEM = pl.BlockSpec(memory_space=pltpu.VMEM)
SMEM = pl.BlockSpec(memory_space=pltpu.SMEM)
HBM = pl.BlockSpec(memory_space=pltpu.HBM)
ANY = pl.BlockSpec(memory_space=pl.ANY)
MIB = 1024 * 1024
PLACE_VMEM = int(52.4 * MIB)
LONG = 10**11


def dot(a, b, dims):
    return lax.dot_general(a, b, (dims, ((), ())), preferred_element_type=F32)


def shape(rows, columns, dtype):
    return jax.ShapeDtypeStruct((rows, columns), dtype)


def call(kernel, outs, in_specs, arrays, scratch=(), flops=0, read=None, vmem=16 * MIB):
    if read is None:
        read = sum(a.size * a.dtype.itemsize for a in arrays)
    return pl.pallas_call(
        kernel,
        out_shape=outs,
        in_specs=in_specs,
        out_specs=[VMEM] * len(outs),
        scratch_shapes=list(scratch),
        compiler_params=pltpu.CompilerParams(vmem_limit_bytes=vmem),
        cost_estimate=pl.CostEstimate(flops=flops, bytes_accessed=read, transcendentals=0),
    )(*arrays)


FAR = 9
NEAR = (0, 3, 5, 7)
OTHER_CORE = 1


def place_kernel(
    docs, ngrams, counts, pmi_hbm, weights_hbm, v_hbm, mine, theirs, v16, pmi, weights, v, sems, v_sem
):
    slots = pmi.shape[0]
    parts = sems.shape[1]
    v_copy = pltpu.make_async_copy(v_hbm, v, v_sem)
    v_copy.start()
    copies = []
    for a, (src, dst) in enumerate(((weights_hbm, weights), (pmi_hbm, pmi))):
        for i in range(parts):
            some = pl.ds(i * (slots // parts), slots // parts)
            copies.append(pltpu.make_async_copy(src.at[0, 0, some], dst.at[some], sems.at[a, i]))
            copies[-1].start()
    half = mine.shape[0] // 2
    me = lax.axis_index("col")
    low, my_z = me & 3, me >> 2
    count = counts[0, 0]
    own = half // 8
    for k in range(slots):
        if k % (slots // parts) == 0:
            for a in range(2):
                copies[a * parts + k // (slots // parts)].wait()
        lanes = pl.ds(pl.multiple_of(ngrams[0, 0, k] * BLK, BLK), BLK)
        z = docs[0, 0, k] ^ my_z
        near, far = z & 1, z >> 1
        live = k < count
        for x in range(2):
            at = pl.multiple_of((far * 4 + near * 2 + x) * own, own)
            core = far ^ (near | x)
            for h, out in enumerate((mine, theirs)):
                rows = pl.ds(pl.multiple_of((low ^ (x * 2 + h) ^ core) * own, own), own)
                tile = weights[k, rows, :]
                out[pl.ds(at, own), lanes] = jnp.where(live, tile, jnp.zeros_like(tile))
                out[pl.ds(at + half, own), lanes] = pmi[k, rows, :]
    v_copy.wait()
    v16[...] = v[...].astype(BF)


def errors_and_gu(u, v_blocks, tiles, e):
    half = u.shape[0]
    gu = None
    for i, v in enumerate(v_blocks):
        width = v.shape[0]
        lanes = slice(i * width, (i + 1) * width)
        s = dot(u, v, ((1,), (1,)))
        w = tiles[:half, lanes].astype(F32)
        p = tiles[half : 2 * half, lanes].astype(F32)
        err = (w * (s - p)).astype(BF)
        e[:, lanes] = err
        term = dot(err, v, ((1,), (0,)))
        gu = term if gu is None else gu + term
    return gu


def pair_kernel(near, other, pair):
    own = near.shape[0]
    pair[:own, :] = near[...].astype(BF)
    pair[own:, :] = other[...].astype(BF)


def rows_kernel(pair, far1, far2, far3, u):
    own = pair.shape[0] // 2
    for x in range(2):
        for z, far in enumerate((pair, far1, far2, far3)):
            at = (x * 4 + z) * own
            u[at : at + own, :] = far[x * own : (x + 1) * own, :]


def all_gu(u, v16, v16_theirs, mine, theirs, e, gv_send, e_theirs):
    n = v16.shape[0] // 2
    gu = errors_and_gu(u[...], [v16[:n], v16[n:]], mine, e)
    gu = gu + errors_and_gu(u[...], [v16_theirs[:n], v16_theirs[n:]], theirs, e_theirs)
    gv_send[...] = dot(e_theirs[...], u[...], ((0,), (0,))).astype(BF)
    return gu


def near_first_kernel(u, *refs):
    *tiles, keep, send1, send2, send3, e, gv_send, e_theirs = refs
    own = u.shape[0] // 8
    gu = all_gu(u, *tiles, e, gv_send, e_theirs)
    for z, out in enumerate((keep, send1, send2, send3)):
        for x in range(2):
            at = (x * 4 + z) * own
            out[x * own : (x + 1) * own, :] = gu[at : at + own].astype(out.dtype)


def far_first_kernel(u, *refs):
    *tiles, keep, send, e, gv_send, e_theirs = refs
    n = keep.shape[0]
    gu = all_gu(u, *tiles, e, gv_send, e_theirs)
    keep[...] = gu[:n]
    send[...] = gu[n:].astype(BF)


def ngram_keep_kernel(e, u, got, ours):
    ours[...] = (dot(e[...], u[...], ((0,), (0,))) + got[...].astype(F32)).astype(BF)


def near_sum_kernel(keep, got1, got2, got3, held, total, total16):
    now = keep[...] + got1[...].astype(F32) + got2[...].astype(F32) + got3[...].astype(F32)
    total[...] = now
    total16[...] = now.astype(BF)


def far_sum_kernel(keep, got, total, send1, send2, send3):
    own = total.shape[0]
    now = keep[...] + got[...].astype(F32)
    for j, out in enumerate((total, send1, send2, send3)):
        out[...] = now[j * own : (j + 1) * own].astype(out.dtype)


def last_kernel(
    doc_rate, ngram_rate, doc, total, got1, got2, got3, ours, ngram_got, v, doc_out, v_out
):
    v_out[...] = v[...] - ngram_rate * (ours[...].astype(F32) + ngram_got[...].astype(F32))
    now = total[...] + got1[...].astype(F32) + got2[...].astype(F32) + got3[...].astype(F32)
    doc_out[...] = doc[...] - doc_rate * now


def pair_update_kernel(rate, doc, other, total, got, doc_out, pair_out):
    own = doc.shape[0]
    now = doc[...] - rate * (total[:own, :] + got[own:, :].astype(F32))
    doc_out[...] = now
    pair_out[:own, :] = now.astype(BF)
    now = other[...] - rate * (total[own:, :] + got[:own, :].astype(F32))
    pair_out[own:, :] = now.astype(BF)


def ngram_update_kernel(rate, ours, got, v, after, v_out, v16):
    now = v[...] - rate * (ours[...].astype(F32) + got[...].astype(F32))
    v_out[...] = now
    v16[...] = now.astype(BF)


def swap(x, mask):
    return lax.ppermute(x, "col", [(i, i ^ mask) for i in range(lax.axis_size("col"))])


def exchange_near(blocks):
    got = [swap(blocks[j - 1], NEAR[j]) for j in (3, 2, 1)]
    return got[::-1]


def swap_group(x):
    return lax.ppermute(x, "grp", [(0, 1), (1, 0)])


def small_slice(doc_now, ngram_now, block_docs, block_ngrams, block_counts, pmi, weights, rates):
    doc_rate, ngram_rate = rates
    own = doc_now.shape[0]
    half = 8 * own
    n = ngram_now.shape[0]
    slots = pmi.shape[2]
    flops = 2 * 2 * half * 2 * n * R

    other = swap(doc_now, FAR)
    mine, theirs, v16 = call(
        place_kernel,
        [shape(2 * half, n, BF), shape(2 * half, n, BF), shape(n, R, BF)],
        [SMEM] * 3 + [HBM] * 3,
        (block_docs, block_ngrams, block_counts, pmi, weights, ngram_now),
        [
            pltpu.VMEM((slots, BLK, BLK), BF),
            pltpu.VMEM((slots, BLK, BLK), BF),
            pltpu.VMEM((n, R), F32),
            pltpu.SemaphoreType.DMA((2, 4)),
            pltpu.SemaphoreType.DMA,
        ],
        vmem=PLACE_VMEM,
    )
    theirs, other = lax.optimization_barrier((theirs, other))
    (pair,) = call(pair_kernel, [shape(2 * own, R, BF)], [VMEM] * 2, (doc_now, other))
    far = exchange_near([pair] * 3)
    theirs = swap(theirs, OTHER_CORE)
    v16_theirs = swap(v16, OTHER_CORE)
    def gradients(kernel, keep_and_send, pair, far, v16, v16_theirs):
        (u,) = call(rows_kernel, [shape(half, R, BF)], [VMEM] * 4, (pair, *far), flops=LONG)
        *outs, e, gv = call(
            kernel,
            keep_and_send + [shape(half, n, BF), shape(n, R, BF)],
            [VMEM] * 5,
            (u, v16, v16_theirs, mine, theirs),
            [pltpu.VMEM((half, n), BF)],
            flops=flops,
        )
        (ours,) = call(
            ngram_keep_kernel,
            [shape(n, R, BF)],
            [VMEM] * 3,
            (e, u, swap(gv, OTHER_CORE)),
            flops=flops // 4,
        )
        return *outs, ours, swap_group(ours)

    keep, *send, ours, ngram_got = gradients(
        near_first_kernel,
        [shape(2 * own, R, F32)] + [shape(2 * own, R, BF)] * 3,
        pair,
        far,
        v16,
        v16_theirs,
    )
    got = exchange_near(send)
    total, total16 = call(
        near_sum_kernel,
        [shape(2 * own, R, F32), shape(2 * own, R, BF)],
        [VMEM] * 4 + [ANY],
        (keep, *got[::-1], theirs),
        flops=LONG,
    )
    doc_now, pair = call(
        functools.partial(pair_update_kernel, doc_rate),
        [shape(own, R, F32), shape(2 * own, R, BF)],
        [VMEM] * 4,
        (doc_now, other, total, swap(total16, FAR)),
    )
    far = exchange_near([pair] * 3)
    ngram_now, v16 = call(
        functools.partial(ngram_update_kernel, ngram_rate),
        [shape(n, R, F32), shape(n, R, BF)],
        [VMEM] * 3 + [ANY],
        (ours, ngram_got, ngram_now, pair),
    )
    v16_theirs = swap(v16, OTHER_CORE)

    keep, send, ours, ngram_got = gradients(
        far_first_kernel,
        [shape(half // 2, R, F32), shape(half // 2, R, BF)],
        pair,
        far,
        v16,
        v16_theirs,
    )
    total, *send = call(
        far_sum_kernel,
        [shape(own, R, F32)] + [shape(own, R, BF)] * 3,
        [VMEM] * 2,
        (keep, swap(send, FAR)),
        flops=LONG,
    )
    return call(
        functools.partial(last_kernel, doc_rate, ngram_rate),
        [shape(own, R, F32), shape(n, R, F32)],
        [VMEM] * 8,
        (doc_now, total, *exchange_near(send)[::-1], ours, ngram_got, ngram_now),
        read=0,
    )


def plain_kernel(docs, ngrams, counts, pmi, weights, u, v, gu, gv, s, e):
    v16 = v[...].astype(BF)
    s[...] = dot(u[...], v16, ((1,), (1,)))
    count = counts[0, 0]
    for k in range(pmi.shape[2]):
        rows = pl.ds(pl.multiple_of(docs[0, 0, k] * BLK, BLK), BLK)
        lanes = pl.ds(pl.multiple_of(ngrams[0, 0, k] * BLK, BLK), BLK)
        live = (k < count).astype(F32)
        p = pmi[0, 0, k].astype(F32)
        w = weights[0, 0, k].astype(F32)
        e[rows, lanes] = (live * w * (s[rows, lanes] - p)).astype(BF)
    gu[...] = dot(e[...], v16, ((1,), (0,)))
    gv[...] = dot(e[...], u[...], ((0,), (0,)))


def any_slice(doc_now, ngram_now, block_docs, block_ngrams, block_counts, pmi, weights, rates):
    doc_rate, ngram_rate = rates
    slots = (block_docs, block_ngrams, block_counts, pmi, weights)
    rows = doc_now.shape[0] * lax.axis_size("col")
    n = ngram_now.shape[0]
    for step in range(2):
        u = lax.all_gather(doc_now.astype(BF), "col", axis=0, tiled=True)
        gu, gv = call(
            plain_kernel,
            [shape(rows, R, F32), shape(n, R, F32)],
            [SMEM] * 3 + [VMEM] * 4,
            (*slots, u, ngram_now),
            [pltpu.VMEM((rows, n), F32), pltpu.VMEM((rows, n), BF)],
            flops=6 * rows * n * R,
        )
        doc_now = doc_now - doc_rate * lax.psum_scatter(gu, "col", scatter_dimension=0, tiled=True)
        ngram_now = ngram_now - ngram_rate * lax.psum(gv, "grp")
    return doc_now, ngram_now


def shards(doc_factors, ngram_factors, block_docs, block_ngrams, block_counts, pmi, weights):
    shard_count = lax.axis_size("col")
    group_count = lax.axis_size("grp")
    doc_total = doc_factors.shape[0] * shard_count * group_count
    ngram_total = ngram_factors.shape[0] * shard_count
    width = doc_factors.shape[1]
    doc_base = math.sqrt(ngram_total) + 1.5 * math.sqrt(width)
    ngram_base = math.sqrt(doc_total) + 1.5 * math.sqrt(width)
    rates = (100.0 / (doc_base * doc_base), 100.0 / (ngram_base * ngram_base))
    run = small_slice if (group_count, shard_count) == (2, 16) else any_slice
    return run(
        doc_factors, ngram_factors, block_docs, block_ngrams, block_counts, pmi, weights, rates
    )


def solution(mesh):
    return jax.shard_map(
        shards,
        mesh=mesh,
        in_specs=(
            P(("grp", "col"), None),
            P("col", None),
            P("grp", "col", None),
            P("grp", "col", None),
            P("grp", "col"),
            P("grp", "col", None, None, None),
            P("grp", "col", None, None, None),
        ),
        out_specs=(P(("grp", "col"), None), P("col", None)),
        check_vma=False,
    )
```

```python
import functools
import math

import jax
import jax.numpy as jnp
from jax import lax
from jax.experimental import pallas as pl
from jax.experimental.pallas import tpu as pltpu
from jax.sharding import PartitionSpec as P

R = 256
BLK = 128
BF = jnp.bfloat16
F32 = jnp.float32
VMEM = pl.BlockSpec(memory_space=pltpu.VMEM)
SMEM = pl.BlockSpec(memory_space=pltpu.SMEM)
HBM = pl.BlockSpec(memory_space=pltpu.HBM)
ANY = pl.BlockSpec(memory_space=pl.ANY)
MIB = 1024 * 1024
PLACE_VMEM = int(52.4 * MIB)
LONG = 10**11


def dot(a, b, dims):
    return lax.dot_general(a, b, (dims, ((), ())), preferred_element_type=F32)


def shape(rows, columns, dtype):
    return jax.ShapeDtypeStruct((rows, columns), dtype)


def call(kernel, outs, in_specs, arrays, scratch=(), flops=0, read=None, vmem=16 * MIB):
    if read is None:
        read = sum(a.size * a.dtype.itemsize for a in arrays)
    return pl.pallas_call(
        kernel,
        out_shape=outs,
        in_specs=in_specs,
        out_specs=[VMEM] * len(outs),
        scratch_shapes=list(scratch),
        compiler_params=pltpu.CompilerParams(vmem_limit_bytes=vmem),
        cost_estimate=pl.CostEstimate(flops=flops, bytes_accessed=read, transcendentals=0),
    )(*arrays)


FAR = 9
NEAR = (0, 3, 5, 7)
OTHER_CORE = 1


def place_kernel(
    docs, ngrams, counts, pmi_hbm, weights_hbm, v_hbm, mine, theirs, v16, pmi, weights, v, sems, v_sem
):
    slots = pmi.shape[0]
    parts = sems.shape[1]
    v_copy = pltpu.make_async_copy(v_hbm, v, v_sem)
    v_copy.start()
    copies = []
    for a, (src, dst) in enumerate(((weights_hbm, weights), (pmi_hbm, pmi))):
        for i in range(parts):
            some = pl.ds(i * (slots // parts), slots // parts)
            copies.append(pltpu.make_async_copy(src.at[0, 0, some], dst.at[some], sems.at[a, i]))
            copies[-1].start()
    half = mine.shape[0] // 2
    me = lax.axis_index("col")
    low, my_z = me & 3, me >> 2
    count = counts[0, 0]
    own = half // 8
    for k in range(slots):
        if k % (slots // parts) == 0:
            for a in range(2):
                copies[a * parts + k // (slots // parts)].wait()
        lanes = pl.ds(pl.multiple_of(ngrams[0, 0, k] * BLK, BLK), BLK)
        z = docs[0, 0, k] ^ my_z
        near, far = z & 1, z >> 1
        live = k < count
        for x in range(2):
            at = pl.multiple_of((far * 4 + near * 2 + x) * own, own)
            core = far ^ (near | x)
            for h, out in enumerate((mine, theirs)):
                rows = pl.ds(pl.multiple_of((low ^ (x * 2 + h) ^ core) * own, own), own)
                tile = weights[k, rows, :]
                out[pl.ds(at, own), lanes] = jnp.where(live, tile, jnp.zeros_like(tile))
                out[pl.ds(at + half, own), lanes] = pmi[k, rows, :]
    v_copy.wait()
    v16[...] = v[...].astype(BF)


def errors_and_gu(u, v_blocks, tiles, e):
    half = u.shape[0]
    gu = None
    for i, v in enumerate(v_blocks):
        width = v.shape[0]
        lanes = slice(i * width, (i + 1) * width)
        s = dot(u, v, ((1,), (1,)))
        w = tiles[:half, lanes].astype(F32)
        p = tiles[half : 2 * half, lanes].astype(F32)
        err = (w * (s - p)).astype(BF)
        e[:, lanes] = err
        term = dot(err, v, ((1,), (0,)))
        gu = term if gu is None else gu + term
    return gu


def pair_kernel(near, other, pair):
    own = near.shape[0]
    pair[:own, :] = near[...].astype(BF)
    pair[own:, :] = other[...].astype(BF)


def rows_kernel(pair, far1, far2, far3, u):
    own = pair.shape[0] // 2
    for x in range(2):
        for z, far in enumerate((pair, far1, far2, far3)):
            at = (x * 4 + z) * own
            u[at : at + own, :] = far[x * own : (x + 1) * own, :]


def all_gu(u, v16, v16_theirs, mine, theirs, e, gv_send, e_theirs):
    n = v16.shape[0] // 2
    gu = errors_and_gu(u[...], [v16[:n], v16[n:]], mine, e)
    gu = gu + errors_and_gu(u[...], [v16_theirs[:n], v16_theirs[n:]], theirs, e_theirs)
    gv_send[...] = dot(e_theirs[...], u[...], ((0,), (0,))).astype(BF)
    return gu


def near_first_kernel(u, *refs):
    *tiles, keep, send1, send2, send3, e, gv_send, e_theirs = refs
    own = u.shape[0] // 8
    gu = all_gu(u, *tiles, e, gv_send, e_theirs)
    for z, out in enumerate((keep, send1, send2, send3)):
        for x in range(2):
            at = (x * 4 + z) * own
            out[x * own : (x + 1) * own, :] = gu[at : at + own].astype(out.dtype)


def far_first_kernel(u, *refs):
    *tiles, keep, send, e, gv_send, e_theirs = refs
    n = keep.shape[0]
    gu = all_gu(u, *tiles, e, gv_send, e_theirs)
    keep[...] = gu[:n]
    send[...] = gu[n:].astype(BF)


def ngram_keep_kernel(e, u, got, ours):
    ours[...] = (dot(e[...], u[...], ((0,), (0,))) + got[...].astype(F32)).astype(BF)


def ngram_part_kernel(e, u, part):
    @pl.when(lax.axis_index("col") < 8)
    def _():
        part[...] = dot(e[...], u[...], ((0,), (0,)))


def ngram_rest_kernel(e, u, part, got, ours):
    ahead = lax.axis_index("col") < 8

    @pl.when(ahead)
    def _():
        ours[...] = (part[...] + got[...].astype(F32)).astype(BF)

    @pl.when(jnp.logical_not(ahead))
    def _():
        ngram_keep_kernel(e, u, got, ours)


def near_sum_kernel(keep, got1, got2, got3, held, total, total16):
    now = keep[...] + got1[...].astype(F32) + got2[...].astype(F32) + got3[...].astype(F32)
    total[...] = now
    total16[...] = now.astype(BF)


def far_sum_kernel(keep, got, total, send1, send2, send3):
    own = total.shape[0]
    now = keep[...] + got[...].astype(F32)
    for j, out in enumerate((total, send1, send2, send3)):
        out[...] = now[j * own : (j + 1) * own].astype(out.dtype)


def last_kernel(
    doc_rate, ngram_rate, doc, total, got1, got2, got3, ours, ngram_got, v, doc_out, v_out
):
    v_out[...] = v[...] - ngram_rate * (ours[...].astype(F32) + ngram_got[...].astype(F32))
    now = total[...] + got1[...].astype(F32) + got2[...].astype(F32) + got3[...].astype(F32)
    doc_out[...] = doc[...] - doc_rate * now


def pair_update_kernel(rate, doc, other, total, got, doc_out, pair_out):
    own = doc.shape[0]
    now = doc[...] - rate * (total[:own, :] + got[own:, :].astype(F32))
    doc_out[...] = now
    pair_out[:own, :] = now.astype(BF)
    now = other[...] - rate * (total[own:, :] + got[:own, :].astype(F32))
    pair_out[own:, :] = now.astype(BF)


def ngram_update_kernel(rate, ours, got, v, after, v_out, v16):
    now = v[...] - rate * (ours[...].astype(F32) + got[...].astype(F32))
    v_out[...] = now
    v16[...] = now.astype(BF)


def swap(x, mask):
    return lax.ppermute(x, "col", [(i, i ^ mask) for i in range(lax.axis_size("col"))])


def exchange_near(blocks):
    got = [swap(blocks[j - 1], NEAR[j]) for j in (3, 2, 1)]
    return got[::-1]


def swap_group(x):
    return lax.ppermute(x, "grp", [(0, 1), (1, 0)])


def small_slice(doc_now, ngram_now, block_docs, block_ngrams, block_counts, pmi, weights, rates):
    doc_rate, ngram_rate = rates
    own = doc_now.shape[0]
    half = 8 * own
    n = ngram_now.shape[0]
    slots = pmi.shape[2]
    flops = 2 * 2 * half * 2 * n * R

    other = swap(doc_now, FAR)
    mine, theirs, v16 = call(
        place_kernel,
        [shape(2 * half, n, BF), shape(2 * half, n, BF), shape(n, R, BF)],
        [SMEM] * 3 + [HBM] * 3,
        (block_docs, block_ngrams, block_counts, pmi, weights, ngram_now),
        [
            pltpu.VMEM((slots, BLK, BLK), BF),
            pltpu.VMEM((slots, BLK, BLK), BF),
            pltpu.VMEM((n, R), F32),
            pltpu.SemaphoreType.DMA((2, 4)),
            pltpu.SemaphoreType.DMA,
        ],
        vmem=PLACE_VMEM,
    )
    theirs, other = lax.optimization_barrier((theirs, other))
    (pair,) = call(pair_kernel, [shape(2 * own, R, BF)], [VMEM] * 2, (doc_now, other))
    far = exchange_near([pair] * 3)
    theirs = swap(theirs, OTHER_CORE)
    v16_theirs = swap(v16, OTHER_CORE)

    def gradients(kernel, keep_and_send, pair, far, v16, v16_theirs):
        (u,) = call(rows_kernel, [shape(half, R, BF)], [VMEM] * 4, (pair, *far), flops=LONG)
        *outs, e, gv = call(
            kernel,
            keep_and_send + [shape(half, n, BF), shape(n, R, BF)],
            [VMEM] * 5,
            (u, v16, v16_theirs, mine, theirs),
            [pltpu.VMEM((half, n), BF)],
            flops=flops,
        )
        got = swap(gv, OTHER_CORE)
        if kernel is near_first_kernel:
            (ours,) = call(
                ngram_keep_kernel, [shape(n, R, BF)], [VMEM] * 3, (e, u, got), flops=flops // 4
            )
        else:
            (part,) = call(
                ngram_part_kernel, [shape(n, R, F32)], [VMEM] * 2, (e, u), flops=flops // 4
            )
            outs[1], part = lax.optimization_barrier((outs[1], part))
            (ours,) = call(
                ngram_rest_kernel, [shape(n, R, BF)], [VMEM] * 4, (e, u, part, got), flops=flops // 4
            )
        return *outs, ours, swap_group(ours)

    keep, *send, ours, ngram_got = gradients(
        near_first_kernel,
        [shape(2 * own, R, F32)] + [shape(2 * own, R, BF)] * 3,
        pair,
        far,
        v16,
        v16_theirs,
    )
    got = exchange_near(send)
    total, total16 = call(
        near_sum_kernel,
        [shape(2 * own, R, F32), shape(2 * own, R, BF)],
        [VMEM] * 4 + [ANY],
        (keep, *got[::-1], theirs),
        flops=LONG,
    )
    doc_now, pair = call(
        functools.partial(pair_update_kernel, doc_rate),
        [shape(own, R, F32), shape(2 * own, R, BF)],
        [VMEM] * 4,
        (doc_now, other, total, swap(total16, FAR)),
    )
    far = exchange_near([pair] * 3)
    ngram_now, v16 = call(
        functools.partial(ngram_update_kernel, ngram_rate),
        [shape(n, R, F32), shape(n, R, BF)],
        [VMEM] * 3 + [ANY],
        (ours, ngram_got, ngram_now, pair),
    )
    v16_theirs = swap(v16, OTHER_CORE)

    keep, send, ours, ngram_got = gradients(
        far_first_kernel,
        [shape(half // 2, R, F32), shape(half // 2, R, BF)],
        pair,
        far,
        v16,
        v16_theirs,
    )
    total, *send = call(
        far_sum_kernel,
        [shape(own, R, F32)] + [shape(own, R, BF)] * 3,
        [VMEM] * 2,
        (keep, swap(send, FAR)),
        flops=LONG,
    )
    return call(
        functools.partial(last_kernel, doc_rate, ngram_rate),
        [shape(own, R, F32), shape(n, R, F32)],
        [VMEM] * 8,
        (doc_now, total, *exchange_near(send)[::-1], ours, ngram_got, ngram_now),
        read=0,
    )


def plain_kernel(docs, ngrams, counts, pmi, weights, u, v, gu, gv, s, e):
    v16 = v[...].astype(BF)
    s[...] = dot(u[...], v16, ((1,), (1,)))
    count = counts[0, 0]
    for k in range(pmi.shape[2]):
        rows = pl.ds(pl.multiple_of(docs[0, 0, k] * BLK, BLK), BLK)
        lanes = pl.ds(pl.multiple_of(ngrams[0, 0, k] * BLK, BLK), BLK)
        live = (k < count).astype(F32)
        p = pmi[0, 0, k].astype(F32)
        w = weights[0, 0, k].astype(F32)
        e[rows, lanes] = (live * w * (s[rows, lanes] - p)).astype(BF)
    gu[...] = dot(e[...], v16, ((1,), (0,)))
    gv[...] = dot(e[...], u[...], ((0,), (0,)))


def any_slice(doc_now, ngram_now, block_docs, block_ngrams, block_counts, pmi, weights, rates):
    doc_rate, ngram_rate = rates
    slots = (block_docs, block_ngrams, block_counts, pmi, weights)
    rows = doc_now.shape[0] * lax.axis_size("col")
    n = ngram_now.shape[0]
    for step in range(2):
        u = lax.all_gather(doc_now.astype(BF), "col", axis=0, tiled=True)
        gu, gv = call(
            plain_kernel,
            [shape(rows, R, F32), shape(n, R, F32)],
            [SMEM] * 3 + [VMEM] * 4,
            (*slots, u, ngram_now),
            [pltpu.VMEM((rows, n), F32), pltpu.VMEM((rows, n), BF)],
            flops=6 * rows * n * R,
        )
        doc_now = doc_now - doc_rate * lax.psum_scatter(gu, "col", scatter_dimension=0, tiled=True)
        ngram_now = ngram_now - ngram_rate * lax.psum(gv, "grp")
    return doc_now, ngram_now


def shards(doc_factors, ngram_factors, block_docs, block_ngrams, block_counts, pmi, weights):
    shard_count = lax.axis_size("col")
    group_count = lax.axis_size("grp")
    doc_total = doc_factors.shape[0] * shard_count * group_count
    ngram_total = ngram_factors.shape[0] * shard_count
    width = doc_factors.shape[1]
    doc_base = math.sqrt(ngram_total) + 1.5 * math.sqrt(width)
    ngram_base = math.sqrt(doc_total) + 1.5 * math.sqrt(width)
    rates = (100.0 / (doc_base * doc_base), 100.0 / (ngram_base * ngram_base))
    run = small_slice if (group_count, shard_count) == (2, 16) else any_slice
    return run(
        doc_factors, ngram_factors, block_docs, block_ngrams, block_counts, pmi, weights, rates
    )


def solution(mesh):
    return jax.shard_map(
        shards,
        mesh=mesh,
        in_specs=(
            P(("grp", "col"), None),
            P("col", None),
            P("grp", "col", None),
            P("grp", "col", None),
            P("grp", "col"),
            P("grp", "col", None, None, None),
            P("grp", "col", None, None, None),
        ),
        out_specs=(P(("grp", "col"), None), P("col", None)),
        check_vma=False,
    )
```

```python
import functools
import math

import jax
import jax.numpy as jnp
from jax import lax
from jax.experimental import pallas as pl
from jax.experimental.pallas import tpu as pltpu
from jax.sharding import PartitionSpec as P

R = 256
BLK = 128
BF = jnp.bfloat16
F32 = jnp.float32
VMEM = pl.BlockSpec(memory_space=pltpu.VMEM)
SMEM = pl.BlockSpec(memory_space=pltpu.SMEM)
HBM = pl.BlockSpec(memory_space=pltpu.HBM)
ANY = pl.BlockSpec(memory_space=pl.ANY)
MIB = 1024 * 1024
PLACE_VMEM = int(52.4 * MIB)
LONG = 10**11


def dot(a, b, dims):
    return lax.dot_general(a, b, (dims, ((), ())), preferred_element_type=F32)


def shape(rows, columns, dtype):
    return jax.ShapeDtypeStruct((rows, columns), dtype)


def call(kernel, outs, in_specs, arrays, scratch=(), flops=0, read=None, vmem=16 * MIB):
    if read is None:
        read = sum(a.size * a.dtype.itemsize for a in arrays)
    return pl.pallas_call(
        kernel,
        out_shape=outs,
        in_specs=in_specs,
        out_specs=[VMEM] * len(outs),
        scratch_shapes=list(scratch),
        compiler_params=pltpu.CompilerParams(vmem_limit_bytes=vmem),
        cost_estimate=pl.CostEstimate(flops=flops, bytes_accessed=read, transcendentals=0),
    )(*arrays)


FAR = 9
NEAR = (0, 3, 5, 6)
OTHER_CORE = 1


def place_kernel(
    docs, ngrams, counts, pmi_hbm, weights_hbm, v_hbm, mine, theirs, v16, pmi, weights, v, sems, v_sem
):
    slots = pmi.shape[0]
    parts = sems.shape[1]
    v_copy = pltpu.make_async_copy(v_hbm, v, v_sem)
    v_copy.start()
    copies = []
    for a, (src, dst) in enumerate(((weights_hbm, weights), (pmi_hbm, pmi))):
        for i in range(parts):
            some = pl.ds(i * (slots // parts), slots // parts)
            copies.append(pltpu.make_async_copy(src.at[0, 0, some], dst.at[some], sems.at[a, i]))
            copies[-1].start()
    half = mine.shape[0] // 2
    me = lax.axis_index("col")
    low, my_z = me & 3, me >> 2
    count = counts[0, 0]
    own = half // 8
    for k in range(slots):
        if k % (slots // parts) == 0:
            for a in range(2):
                copies[a * parts + k // (slots // parts)].wait()
        lanes = pl.ds(pl.multiple_of(ngrams[0, 0, k] * BLK, BLK), BLK)
        z = docs[0, 0, k] ^ my_z
        near, far = z & 1, z >> 1
        live = k < count
        for x in range(2):
            at = pl.multiple_of((far * 4 + near * 2 + x) * own, own)
            core = far ^ near ^ x
            for h, out in enumerate((mine, theirs)):
                rows = pl.ds(pl.multiple_of((low ^ (x * 2 + h) ^ core) * own, own), own)
                tile = weights[k, rows, :]
                out[pl.ds(at, own), lanes] = jnp.where(live, tile, jnp.zeros_like(tile))
                out[pl.ds(at + half, own), lanes] = pmi[k, rows, :]
    v_copy.wait()
    v16[...] = v[...].astype(BF)


def errors_and_gu(u, v_blocks, tiles, e):
    half = u.shape[0]
    gu = None
    for i, v in enumerate(v_blocks):
        width = v.shape[0]
        lanes = slice(i * width, (i + 1) * width)
        s = dot(u, v, ((1,), (1,)))
        w = tiles[:half, lanes].astype(F32)
        p = tiles[half : 2 * half, lanes].astype(F32)
        err = (w * (s - p)).astype(BF)
        e[:, lanes] = err
        term = dot(err, v, ((1,), (0,)))
        gu = term if gu is None else gu + term
    return gu


def pair_kernel(near, other, pair):
    own = near.shape[0]
    pair[:own, :] = near[...].astype(BF)
    pair[own:, :] = other[...].astype(BF)


def rows_kernel(pair, far1, far2, far3, u):
    own = pair.shape[0] // 2
    for x in range(2):
        for z, far in enumerate((pair, far1, far2, far3)):
            at = (x * 4 + z) * own
            u[at : at + own, :] = far[x * own : (x + 1) * own, :]


def all_gu(u, v16, v16_theirs, mine, theirs, e, gv_send, e_theirs):
    n = v16.shape[0] // 2
    gu = errors_and_gu(u[...], [v16[:n], v16[n:]], mine, e)
    gu = gu + errors_and_gu(u[...], [v16_theirs[:n], v16_theirs[n:]], theirs, e_theirs)
    gv_send[...] = dot(e_theirs[...], u[...], ((0,), (0,))).astype(BF)
    return gu


def near_kernel(u, *refs):
    *tiles, keep, send1, send2, send3, e, gv_send, e_theirs = refs
    own = u.shape[0] // 8
    gu = all_gu(u, *tiles, e, gv_send, e_theirs)
    for z, out in enumerate((keep, send1, send2, send3)):
        for x in range(2):
            at = (x * 4 + z) * own
            out[x * own : (x + 1) * own, :] = gu[at : at + own].astype(out.dtype)


def halving_kernel(u, *refs):
    *tiles, keep, send, e, gv_send, e_theirs = refs
    own = u.shape[0] // 8
    gu = all_gu(u, *tiles, e, gv_send, e_theirs)
    for far in range(2):
        at, to = far * 4 * own, slice(far * 2 * own, (far + 1) * 2 * own)
        keep[to, :] = gu[at : at + 2 * own]
        send[to, :] = gu[at + 2 * own : at + 4 * own].astype(BF)


def ngram_keep_kernel(e, u, got, ours):
    ours[...] = (dot(e[...], u[...], ((0,), (0,))) + got[...].astype(F32)).astype(BF)


def near_sum_kernel(keep, got1, got2, got3, held, total, total16):
    now = keep[...] + got1[...].astype(F32) + got2[...].astype(F32) + got3[...].astype(F32)
    total[...] = now
    total16[...] = now.astype(BF)


def halving_sum_kernel(keep, got, total, send):
    n = total.shape[0]
    total[...] = keep[:n, :] + got[:n, :].astype(F32)
    send[...] = (keep[n:, :] + got[n:, :].astype(F32)).astype(BF)


def ngram_last_kernel(rate, ours, got, v, v_out, written):
    written[...] = jnp.zeros_like(written)
    v_out[...] = v[...] - rate * (ours[...].astype(F32) + got[...].astype(F32))


def doc_last_kernel(rate, doc, total, got, after, doc_out):
    doc_out[...] = doc[...] - rate * (total[...] + got[...].astype(F32))


def pair_update_kernel(rate, doc, other, total, got, doc_out, pair_out):
    own = doc.shape[0]
    now = doc[...] - rate * (total[:own, :] + got[own:, :].astype(F32))
    doc_out[...] = now
    pair_out[:own, :] = now.astype(BF)
    now = other[...] - rate * (total[own:, :] + got[:own, :].astype(F32))
    pair_out[own:, :] = now.astype(BF)


def ngram_update_kernel(rate, ours, got, v, after, v_out, v16):
    now = v[...] - rate * (ours[...].astype(F32) + got[...].astype(F32))
    v_out[...] = now
    v16[...] = now.astype(BF)


def swap(x, mask):
    return lax.ppermute(x, "col", [(i, i ^ mask) for i in range(lax.axis_size("col"))])


def exchange_near(blocks):
    got = [swap(blocks[j - 1], NEAR[j]) for j in (3, 2, 1)]
    return got[::-1]


def swap_group(x):
    return lax.ppermute(x, "grp", [(0, 1), (1, 0)])


def small_slice(doc_now, ngram_now, block_docs, block_ngrams, block_counts, pmi, weights, rates):
    doc_rate, ngram_rate = rates
    own = doc_now.shape[0]
    half = 8 * own
    n = ngram_now.shape[0]
    slots = pmi.shape[2]
    flops = 2 * 2 * half * 2 * n * R

    other = swap(doc_now, FAR)
    mine, theirs, v16 = call(
        place_kernel,
        [shape(2 * half, n, BF), shape(2 * half, n, BF), shape(n, R, BF)],
        [SMEM] * 3 + [HBM] * 3,
        (block_docs, block_ngrams, block_counts, pmi, weights, ngram_now),
        [
            pltpu.VMEM((slots, BLK, BLK), BF),
            pltpu.VMEM((slots, BLK, BLK), BF),
            pltpu.VMEM((n, R), F32),
            pltpu.SemaphoreType.DMA((2, 4)),
            pltpu.SemaphoreType.DMA,
        ],
        vmem=PLACE_VMEM,
    )
    theirs, other = lax.optimization_barrier((theirs, other))
    (pair,) = call(pair_kernel, [shape(2 * own, R, BF)], [VMEM] * 2, (doc_now, other))
    far = exchange_near([pair] * 3)
    theirs = swap(theirs, OTHER_CORE)
    v16_theirs = swap(v16, OTHER_CORE)
    def gradients(kernel, keep_and_send, pair, far, v16, v16_theirs):
        (u,) = call(rows_kernel, [shape(half, R, BF)], [VMEM] * 4, (pair, *far), flops=LONG)
        *outs, e, gv = call(
            kernel,
            keep_and_send + [shape(half, n, BF), shape(n, R, BF)],
            [VMEM] * 5,
            (u, v16, v16_theirs, mine, theirs),
            [pltpu.VMEM((half, n), BF)],
            flops=flops,
        )
        (ours,) = call(
            ngram_keep_kernel,
            [shape(n, R, BF)],
            [VMEM] * 3,
            (e, u, swap(gv, OTHER_CORE)),
            flops=flops // 4,
        )
        return *outs, ours, swap_group(ours)

    keep, *send, ours, ngram_got = gradients(
        near_kernel,
        [shape(2 * own, R, F32)] + [shape(2 * own, R, BF)] * 3,
        pair,
        far,
        v16,
        v16_theirs,
    )
    got = exchange_near(send)
    total, total16 = call(
        near_sum_kernel,
        [shape(2 * own, R, F32), shape(2 * own, R, BF)],
        [VMEM] * 4 + [ANY],
        (keep, *got[::-1], theirs),
        flops=LONG,
    )
    doc_now, pair = call(
        functools.partial(pair_update_kernel, doc_rate),
        [shape(own, R, F32), shape(2 * own, R, BF)],
        [VMEM] * 4,
        (doc_now, other, total, swap(total16, FAR)),
    )
    far = exchange_near([pair] * 3)
    ngram_now, v16 = call(
        functools.partial(ngram_update_kernel, ngram_rate),
        [shape(n, R, F32), shape(n, R, BF)],
        [VMEM] * 3 + [ANY],
        (ours, ngram_got, ngram_now, pair),
    )
    v16_theirs = swap(v16, OTHER_CORE)

    total, send, ours, ngram_got = gradients(
        halving_kernel,
        [shape(half // 2, R, F32), shape(half // 2, R, BF)],
        pair,
        far,
        v16,
        v16_theirs,
    )
    for mask, rows, hint in ((NEAR[2], 2 * own, LONG), (FAR, own, 0)):
        total, send = call(
            halving_sum_kernel,
            [shape(rows, R, F32), shape(rows, R, BF)],
            [VMEM] * 2,
            (total, swap(send, mask)),
            flops=hint,
            read=0,
        )
    got = swap(send, NEAR[1])
    ngram_now, written = call(
        functools.partial(ngram_last_kernel, ngram_rate),
        [shape(n, R, F32), shape(8, 128, F32)],
        [VMEM] * 3,
        (ours, ngram_got, ngram_now),
        read=0,
    )
    (doc_now,) = call(
        functools.partial(doc_last_kernel, doc_rate),
        [shape(own, R, F32)],
        [VMEM] * 3 + [ANY],
        (doc_now, total, got, written),
        read=0,
    )
    return doc_now, ngram_now


def plain_kernel(docs, ngrams, counts, pmi, weights, u, v, gu, gv, s, e):
    v16 = v[...].astype(BF)
    s[...] = dot(u[...], v16, ((1,), (1,)))
    count = counts[0, 0]
    for k in range(pmi.shape[2]):
        rows = pl.ds(pl.multiple_of(docs[0, 0, k] * BLK, BLK), BLK)
        lanes = pl.ds(pl.multiple_of(ngrams[0, 0, k] * BLK, BLK), BLK)
        live = (k < count).astype(F32)
        p = pmi[0, 0, k].astype(F32)
        w = weights[0, 0, k].astype(F32)
        e[rows, lanes] = (live * w * (s[rows, lanes] - p)).astype(BF)
    gu[...] = dot(e[...], v16, ((1,), (0,)))
    gv[...] = dot(e[...], u[...], ((0,), (0,)))


def any_slice(doc_now, ngram_now, block_docs, block_ngrams, block_counts, pmi, weights, rates):
    doc_rate, ngram_rate = rates
    slots = (block_docs, block_ngrams, block_counts, pmi, weights)
    rows = doc_now.shape[0] * lax.axis_size("col")
    n = ngram_now.shape[0]
    for step in range(2):
        u = lax.all_gather(doc_now.astype(BF), "col", axis=0, tiled=True)
        gu, gv = call(
            plain_kernel,
            [shape(rows, R, F32), shape(n, R, F32)],
            [SMEM] * 3 + [VMEM] * 4,
            (*slots, u, ngram_now),
            [pltpu.VMEM((rows, n), F32), pltpu.VMEM((rows, n), BF)],
            flops=6 * rows * n * R,
        )
        doc_now = doc_now - doc_rate * lax.psum_scatter(gu, "col", scatter_dimension=0, tiled=True)
        ngram_now = ngram_now - ngram_rate * lax.psum(gv, "grp")
    return doc_now, ngram_now


def shards(doc_factors, ngram_factors, block_docs, block_ngrams, block_counts, pmi, weights):
    shard_count = lax.axis_size("col")
    group_count = lax.axis_size("grp")
    doc_total = doc_factors.shape[0] * shard_count * group_count
    ngram_total = ngram_factors.shape[0] * shard_count
    width = doc_factors.shape[1]
    doc_base = math.sqrt(ngram_total) + 1.5 * math.sqrt(width)
    ngram_base = math.sqrt(doc_total) + 1.5 * math.sqrt(width)
    rates = (100.0 / (doc_base * doc_base), 100.0 / (ngram_base * ngram_base))
    run = small_slice if (group_count, shard_count) == (2, 16) else any_slice
    return run(
        doc_factors, ngram_factors, block_docs, block_ngrams, block_counts, pmi, weights, rates
    )


def solution(mesh):
    return jax.shard_map(
        shards,
        mesh=mesh,
        in_specs=(
            P(("grp", "col"), None),
            P("col", None),
            P("grp", "col", None),
            P("grp", "col", None),
            P("grp", "col"),
            P("grp", "col", None, None, None),
            P("grp", "col", None, None, None),
        ),
        out_specs=(P(("grp", "col"), None), P("col", None)),
        check_vma=False,
    )
```

```python
import functools
import math

import jax
import jax.numpy as jnp
from jax import lax
from jax.experimental import pallas as pl
from jax.experimental.pallas import tpu as pltpu
from jax.sharding import PartitionSpec as P

R = 256
BLK = 128
BF = jnp.bfloat16
F32 = jnp.float32
VMEM = pl.BlockSpec(memory_space=pltpu.VMEM)
SMEM = pl.BlockSpec(memory_space=pltpu.SMEM)
HBM = pl.BlockSpec(memory_space=pltpu.HBM)
ANY = pl.BlockSpec(memory_space=pl.ANY)
MIB = 1024 * 1024
PLACE_VMEM = int(52.4 * MIB)
LONG = 10**11


def dot(a, b, dims):
    return lax.dot_general(a, b, (dims, ((), ())), preferred_element_type=F32)


def shape(rows, columns, dtype):
    return jax.ShapeDtypeStruct((rows, columns), dtype)


def call(kernel, outs, in_specs, arrays, scratch=(), flops=0, read=None, vmem=16 * MIB):
    if read is None:
        read = sum(a.size * a.dtype.itemsize for a in arrays)
    return pl.pallas_call(
        kernel,
        out_shape=outs,
        in_specs=in_specs,
        out_specs=[VMEM] * len(outs),
        scratch_shapes=list(scratch),
        compiler_params=pltpu.CompilerParams(vmem_limit_bytes=vmem),
        cost_estimate=pl.CostEstimate(flops=flops, bytes_accessed=read, transcendentals=0),
    )(*arrays)


FAR = 9
NEAR = (0, 3, 5, 7)
OTHER_CORE = 1


def place_kernel(
    docs_hbm, ngrams_hbm, counts_hbm, pmi_hbm, weights_hbm, v_hbm, mine, theirs, v16,
    docs, ngrams, counts, pmi, weights, v, small_sems, sems, v_sem,
):
    slots = pmi.shape[0]
    parts = sems.shape[1]
    small = [
        pltpu.make_async_copy(src, dst, small_sems.at[i])
        for i, (src, dst) in enumerate(((docs_hbm, docs), (ngrams_hbm, ngrams), (counts_hbm, counts)))
    ]
    for copy in small:
        copy.start()
    copies = []
    for a, (src, dst) in enumerate(((weights_hbm, weights), (pmi_hbm, pmi))):
        for i in range(parts):
            some = pl.ds(i * (slots // parts), slots // parts)
            copies.append(pltpu.make_async_copy(src.at[0, 0, some], dst.at[some], sems.at[a, i]))
            copies[-1].start()
    v_copy = pltpu.make_async_copy(v_hbm, v, v_sem)
    v_copy.start()
    for copy in small:
        copy.wait()
    half = mine.shape[0] // 2
    me = lax.axis_index("col")
    low, my_z = me & 3, me >> 2
    count = counts[0, 0]
    own = half // 8
    for k in range(slots):
        if k % (slots // parts) == 0:
            for a in range(2):
                copies[a * parts + k // (slots // parts)].wait()
        lanes = pl.ds(pl.multiple_of(ngrams[0, 0, k] * BLK, BLK), BLK)
        z = docs[0, 0, k] ^ my_z
        near, far = z & 1, z >> 1
        live = k < count
        for x in range(2):
            at = pl.multiple_of((far * 4 + near * 2 + x) * own, own)
            core = far ^ (near | x)
            for h, out in enumerate((mine, theirs)):
                rows = pl.ds(pl.multiple_of((low ^ (x * 2 + h) ^ core) * own, own), own)
                tile = weights[k, rows, :]
                out[pl.ds(at, own), lanes] = jnp.where(live, tile, jnp.zeros_like(tile))
                out[pl.ds(at + half, own), lanes] = pmi[k, rows, :]
    v_copy.wait()
    v16[...] = v[...].astype(BF)


def errors_and_gu(u, v_blocks, tiles, e):
    half = u.shape[0]
    gu = None
    for i, v in enumerate(v_blocks):
        width = v.shape[0]
        lanes = slice(i * width, (i + 1) * width)
        s = dot(u, v, ((1,), (1,)))
        w = tiles[:half, lanes].astype(F32)
        p = tiles[half : 2 * half, lanes].astype(F32)
        err = (w * (s - p)).astype(BF)
        e[:, lanes] = err
        term = dot(err, v, ((1,), (0,)))
        gu = term if gu is None else gu + term
    return gu


def pair_kernel(near, other, pair):
    own = near.shape[0]
    pair[:own, :] = near[...].astype(BF)
    pair[own:, :] = other[...].astype(BF)


def rows_kernel(pair, far1, far2, far3, u):
    own = pair.shape[0] // 2
    for x in range(2):
        for z, far in enumerate((pair, far1, far2, far3)):
            at = (x * 4 + z) * own
            u[at : at + own, :] = far[x * own : (x + 1) * own, :]


def all_gu(u, v16, v16_theirs, mine, theirs, e, gv_send, e_theirs):
    n = v16.shape[0] // 2
    gu = errors_and_gu(u[...], [v16[:n], v16[n:]], mine, e)
    gu = gu + errors_and_gu(u[...], [v16_theirs[:n], v16_theirs[n:]], theirs, e_theirs)
    gv_send[...] = dot(e_theirs[...], u[...], ((0,), (0,))).astype(BF)
    return gu


def near_first_kernel(u, *refs):
    *tiles, keep, send1, send2, send3, e, gv_send, e_theirs = refs
    own = u.shape[0] // 8
    gu = all_gu(u, *tiles, e, gv_send, e_theirs)
    for z, out in enumerate((keep, send1, send2, send3)):
        for x in range(2):
            at = (x * 4 + z) * own
            out[x * own : (x + 1) * own, :] = gu[at : at + own].astype(out.dtype)


def far_first_kernel(u, *refs):
    *tiles, keep, send, e, gv_send, e_theirs = refs
    n = keep.shape[0]
    gu = all_gu(u, *tiles, e, gv_send, e_theirs)
    keep[...] = gu[:n]
    send[...] = gu[n:].astype(BF)


def ngram_keep_kernel(e, u, got, ours):
    ours[...] = (dot(e[...], u[...], ((0,), (0,))) + got[...].astype(F32)).astype(BF)


def ngram_part_kernel(e, u, part):
    @pl.when(lax.axis_index("col") < 8)
    def _():
        part[...] = dot(e[...], u[...], ((0,), (0,)))


def ngram_rest_kernel(e, u, part, got, ours):
    ahead = lax.axis_index("col") < 8

    @pl.when(ahead)
    def _():
        ours[...] = (part[...] + got[...].astype(F32)).astype(BF)

    @pl.when(jnp.logical_not(ahead))
    def _():
        ngram_keep_kernel(e, u, got, ours)


def near_sum_kernel(keep, got1, got2, got3, held, total, total16):
    now = keep[...] + got1[...].astype(F32) + got2[...].astype(F32) + got3[...].astype(F32)
    total[...] = now
    total16[...] = now.astype(BF)


def far_sum_kernel(keep, got, total, send1, send2, send3):
    own = total.shape[0]
    now = keep[...] + got[...].astype(F32)
    for j, out in enumerate((total, send1, send2, send3)):
        out[...] = now[j * own : (j + 1) * own].astype(out.dtype)


def last_kernel(
    doc_rate, ngram_rate, doc, total, got1, got2, got3, ours, ngram_got, v, doc_out, v_out
):
    v_out[...] = v[...] - ngram_rate * (ours[...].astype(F32) + ngram_got[...].astype(F32))
    now = total[...] + got1[...].astype(F32) + got2[...].astype(F32) + got3[...].astype(F32)
    doc_out[...] = doc[...] - doc_rate * now


def pair_update_kernel(rate, doc, other, total, got, doc_out, pair_out):
    own = doc.shape[0]
    now = doc[...] - rate * (total[:own, :] + got[own:, :].astype(F32))
    doc_out[...] = now
    pair_out[:own, :] = now.astype(BF)
    now = other[...] - rate * (total[own:, :] + got[:own, :].astype(F32))
    pair_out[own:, :] = now.astype(BF)


def ngram_update_kernel(rate, ours, got, v, after, v_out, v16):
    now = v[...] - rate * (ours[...].astype(F32) + got[...].astype(F32))
    v_out[...] = now
    v16[...] = now.astype(BF)


def swap(x, mask):
    return lax.ppermute(x, "col", [(i, i ^ mask) for i in range(lax.axis_size("col"))])


def exchange_near(blocks):
    got = [swap(blocks[j - 1], NEAR[j]) for j in (3, 2, 1)]
    return got[::-1]


def swap_group(x):
    return lax.ppermute(x, "grp", [(0, 1), (1, 0)])


def small_slice(doc_now, ngram_now, block_docs, block_ngrams, block_counts, pmi, weights, rates):
    doc_rate, ngram_rate = rates
    own = doc_now.shape[0]
    half = 8 * own
    n = ngram_now.shape[0]
    slots = pmi.shape[2]
    flops = 2 * 2 * half * 2 * n * R

    other = swap(doc_now, FAR)
    mine, theirs, v16 = call(
        place_kernel,
        [shape(2 * half, n, BF), shape(2 * half, n, BF), shape(n, R, BF)],
        [HBM] * 6,
        (block_docs, block_ngrams, block_counts, pmi, weights, ngram_now),
        [
            pltpu.SMEM(block_docs.shape, jnp.int32),
            pltpu.SMEM(block_ngrams.shape, jnp.int32),
            pltpu.SMEM(block_counts.shape, jnp.int32),
            pltpu.VMEM((slots, BLK, BLK), BF),
            pltpu.VMEM((slots, BLK, BLK), BF),
            pltpu.VMEM((n, R), F32),
            pltpu.SemaphoreType.DMA((3,)),
            pltpu.SemaphoreType.DMA((2, 4)),
            pltpu.SemaphoreType.DMA,
        ],
        vmem=PLACE_VMEM,
    )
    theirs, other = lax.optimization_barrier((theirs, other))
    (pair,) = call(pair_kernel, [shape(2 * own, R, BF)], [VMEM] * 2, (doc_now, other))
    far = exchange_near([pair] * 3)
    theirs = swap(theirs, OTHER_CORE)
    v16_theirs = swap(v16, OTHER_CORE)

    def gradients(kernel, keep_and_send, pair, far, v16, v16_theirs):
        (u,) = call(rows_kernel, [shape(half, R, BF)], [VMEM] * 4, (pair, *far), flops=LONG)
        *outs, e, gv = call(
            kernel,
            keep_and_send + [shape(half, n, BF), shape(n, R, BF)],
            [VMEM] * 5,
            (u, v16, v16_theirs, mine, theirs),
            [pltpu.VMEM((half, n), BF)],
            flops=flops,
        )
        got = swap(gv, OTHER_CORE)
        if kernel is near_first_kernel:
            (ours,) = call(
                ngram_keep_kernel, [shape(n, R, BF)], [VMEM] * 3, (e, u, got), flops=flops // 4
            )
        else:
            (part,) = call(
                ngram_part_kernel, [shape(n, R, F32)], [VMEM] * 2, (e, u), flops=flops // 4
            )
            outs[1], part = lax.optimization_barrier((outs[1], part))
            (ours,) = call(
                ngram_rest_kernel, [shape(n, R, BF)], [VMEM] * 4, (e, u, part, got), flops=flops // 4
            )
        return *outs, ours, swap_group(ours)

    keep, *send, ours, ngram_got = gradients(
        near_first_kernel,
        [shape(2 * own, R, F32)] + [shape(2 * own, R, BF)] * 3,
        pair,
        far,
        v16,
        v16_theirs,
    )
    got = exchange_near(send)
    total, total16 = call(
        near_sum_kernel,
        [shape(2 * own, R, F32), shape(2 * own, R, BF)],
        [VMEM] * 4 + [ANY],
        (keep, *got[::-1], theirs),
        flops=LONG,
    )
    doc_now, pair = call(
        functools.partial(pair_update_kernel, doc_rate),
        [shape(own, R, F32), shape(2 * own, R, BF)],
        [VMEM] * 4,
        (doc_now, other, total, swap(total16, FAR)),
    )
    far = exchange_near([pair] * 3)
    ngram_now, v16 = call(
        functools.partial(ngram_update_kernel, ngram_rate),
        [shape(n, R, F32), shape(n, R, BF)],
        [VMEM] * 3 + [ANY],
        (ours, ngram_got, ngram_now, pair),
    )
    v16_theirs = swap(v16, OTHER_CORE)

    keep, send, ours, ngram_got = gradients(
        far_first_kernel,
        [shape(half // 2, R, F32), shape(half // 2, R, BF)],
        pair,
        far,
        v16,
        v16_theirs,
    )
    total, *send = call(
        far_sum_kernel,
        [shape(own, R, F32)] + [shape(own, R, BF)] * 3,
        [VMEM] * 2,
        (keep, swap(send, FAR)),
        flops=LONG,
    )
    return call(
        functools.partial(last_kernel, doc_rate, ngram_rate),
        [shape(own, R, F32), shape(n, R, F32)],
        [VMEM] * 8,
        (doc_now, total, *exchange_near(send)[::-1], ours, ngram_got, ngram_now),
        read=0,
    )


def plain_kernel(docs, ngrams, counts, pmi, weights, u, v, gu, gv, s, e):
    v16 = v[...].astype(BF)
    s[...] = dot(u[...], v16, ((1,), (1,)))
    count = counts[0, 0]
    for k in range(pmi.shape[2]):
        rows = pl.ds(pl.multiple_of(docs[0, 0, k] * BLK, BLK), BLK)
        lanes = pl.ds(pl.multiple_of(ngrams[0, 0, k] * BLK, BLK), BLK)
        live = (k < count).astype(F32)
        p = pmi[0, 0, k].astype(F32)
        w = weights[0, 0, k].astype(F32)
        e[rows, lanes] = (live * w * (s[rows, lanes] - p)).astype(BF)
    gu[...] = dot(e[...], v16, ((1,), (0,)))
    gv[...] = dot(e[...], u[...], ((0,), (0,)))


def any_slice(doc_now, ngram_now, block_docs, block_ngrams, block_counts, pmi, weights, rates):
    doc_rate, ngram_rate = rates
    slots = (block_docs, block_ngrams, block_counts, pmi, weights)
    rows = doc_now.shape[0] * lax.axis_size("col")
    n = ngram_now.shape[0]
    for step in range(2):
        u = lax.all_gather(doc_now.astype(BF), "col", axis=0, tiled=True)
        gu, gv = call(
            plain_kernel,
            [shape(rows, R, F32), shape(n, R, F32)],
            [SMEM] * 3 + [VMEM] * 4,
            (*slots, u, ngram_now),
            [pltpu.VMEM((rows, n), F32), pltpu.VMEM((rows, n), BF)],
            flops=6 * rows * n * R,
        )
        doc_now = doc_now - doc_rate * lax.psum_scatter(gu, "col", scatter_dimension=0, tiled=True)
        ngram_now = ngram_now - ngram_rate * lax.psum(gv, "grp")
    return doc_now, ngram_now


def shards(doc_factors, ngram_factors, block_docs, block_ngrams, block_counts, pmi, weights):
    shard_count = lax.axis_size("col")
    group_count = lax.axis_size("grp")
    doc_total = doc_factors.shape[0] * shard_count * group_count
    ngram_total = ngram_factors.shape[0] * shard_count
    width = doc_factors.shape[1]
    doc_base = math.sqrt(ngram_total) + 1.5 * math.sqrt(width)
    ngram_base = math.sqrt(doc_total) + 1.5 * math.sqrt(width)
    rates = (100.0 / (doc_base * doc_base), 100.0 / (ngram_base * ngram_base))
    run = small_slice if (group_count, shard_count) == (2, 16) else any_slice
    return run(
        doc_factors, ngram_factors, block_docs, block_ngrams, block_counts, pmi, weights, rates
    )


def solution(mesh):
    return jax.shard_map(
        shards,
        mesh=mesh,
        in_specs=(
            P(("grp", "col"), None),
            P("col", None),
            P("grp", "col", None),
            P("grp", "col", None),
            P("grp", "col"),
            P("grp", "col", None, None, None),
            P("grp", "col", None, None, None),
        ),
        out_specs=(P(("grp", "col"), None), P("col", None)),
        check_vma=False,
    )
```
